512 devices in a mesh: dp: 64 (over x, z), tensor: 8 (over y, core).
Axes of the slice: x: 4, y: 4, z: 16, core: 2. Of those that a mesh axis runs over, the one named last changes fastest.
Arguments:
- hidden: bfloat16 [8192, 5120], P('dp', 'tensor'), may hold values from -6 to 6
- queries: bfloat16 [8192, 8192], P('dp', 'tensor'), may hold values from -21 to 21
- out_grad: bfloat16 [8192, 8192], P('dp', 'tensor'), may hold values from -16 to 16
- w_key: bfloat16 [5120, 1024], P(None, 'tensor'), may hold values from -0.078125 to 0.078125
- w_value: bfloat16 [5120, 1024], P(None, 'tensor'), may hold values from -0.078125 to 0.078125
- prompt_kv: bfloat16 [64, 2, 1024, 1024], P('dp', None, None, 'tensor'), may hold values from -6 to 6
- block_dest: int32 [64], replicated, may hold values from 0 to 63, as said below
- resp_len: int32 [64], replicated, may hold values from 1 to 128, as said below
Outputs:
- grad_query: bfloat16 [8192, 8192], P('dp', 'tensor')
- grad_hidden: bfloat16 [8192, 5120], P('dp', 'tensor')
- grad_prompt_kv: bfloat16 [64, 2, 1024, 1024], P('dp', None, None, 'tensor')
The draws below stay inside these ranges and needn't reach their ends.
Inputs may be any that keep to these rules, and one draw needn't show every extreme that they name: block_dest[b] // 4 == b // 4; no shard is the destination of more than 3 blocks, and in every draw some shard is the destination of exactly 3. `resp_len`: some block is full in every draw.
All inputs are finite; a program needn't handle non-finite values.
Results may differ from the reference program's by a relative error of at most 0.019.
Values may be sent and summed in bfloat16 or wider, within the bound.
A program may use at most 64 MiB of HBM per device.

```python
import math
import jax
import jax.numpy as jnp
from jax import lax

D = 5120
HQ = 64
KVH = 8
HD = 128
PL = 1024
BT = 128
GROUP = 4
CAP = 3
NB = 64


def shard_routes(key):
    groups = NB // GROUP
    group_keys = jax.random.split(jax.random.fold_in(key, 11), groups)
    shuffled = jax.vmap(lambda one_key: jax.random.permutation(one_key, GROUP))(group_keys)
    counts = jax.random.randint(jax.random.fold_in(key, 12), (groups,), 1, CAP + 1)
    chosen = jax.random.randint(jax.random.fold_in(key, 13), (), 0, groups - 1)
    counts = jnp.where(jnp.arange(groups) == chosen, CAP, counts)
    rank_local = jnp.argsort(shuffled, axis=1)
    hot_shard = shuffled[:, :1]
    local_ids = jnp.arange(GROUP)[None, :]
    dest_local = jnp.where(rank_local < counts[:, None], hot_shard, local_ids)
    last_pattern = jnp.array([0, GROUP - 1, GROUP - 1, 0], jnp.int32)[None, :]
    is_last = (jnp.arange(groups) == groups - 1)[:, None]
    dest_local = jnp.where(is_last, last_pattern, dest_local)
    middle_group = NB // 2 // GROUP
    upper_pattern = jnp.array([0, 0, 0, GROUP - 1], jnp.int32)[None, :]
    lower_pattern = jnp.array([0, 1, 2, 0], jnp.int32)[None, :]
    is_upper = (jnp.arange(groups) == middle_group)[:, None]
    is_lower = (jnp.arange(groups) == middle_group - 1)[:, None]
    dest_local = jnp.where(is_upper, upper_pattern, dest_local)
    dest_local = jnp.where(is_lower, lower_pattern, dest_local)
    return (dest_local + jnp.arange(groups)[:, None] * GROUP).reshape(NB).astype(jnp.int32)


def draw_block_dest(key, part):
    return shard_routes(key)


def draw_resp_len(key, part):
    key = jax.random.fold_in(key, 2)
    lengths = jax.random.randint(jax.random.fold_in(key, 1), (NB,), 1, BT + 1)
    chosen = jax.random.randint(jax.random.fold_in(key, 2), (), 0, NB)
    return jnp.where(jnp.arange(NB) == chosen, BT, lengths).astype(jnp.int32)


def draw_prompt_kv(key, part):
    key = jax.random.fold_in(key, 3)
    draw_dims = (NB, 2, PL, KVH * HD)
    base_draw = jax.random.truncated_normal(key, -6.0, 6.0, draw_dims, jnp.float32)
    return base_draw.astype(jnp.bfloat16)


def draw_queries(key, part):
    key = jax.random.fold_in(key, 4)
    draw_dims = (NB * BT, HQ * HD)
    base_draw = jax.random.truncated_normal(key, -6.0, 6.0, draw_dims, jnp.float32)
    return base_draw.astype(jnp.bfloat16)


def block_levels(stream_key, shape, cuts, least, high):
    factor_of, own = 1.0, jax.random.fold_in(stream_key, 6)
    for axis_at, shards_of in cuts:
        draws = jnp.exp(jax.random.uniform(jax.random.fold_in(own, axis_at), (shards_of,), jnp.float32, least / len(cuts), high / len(cuts)))
        factor_of = factor_of * jnp.repeat(draws, shape[axis_at] // shards_of).reshape([-1 if axis == axis_at else 1 for axis in range(len(shape))])
    return factor_of


def bell_draw(own_key, extent, deviation, limit, pieces=(), held_as=jnp.bfloat16):
    result = jax.random.normal(own_key, extent, jnp.float32) * deviation
    if len(pieces) > 0:
        result = block_levels(own_key, extent, pieces, -0.22, 0.18) * result
    return jnp.clip(result, min=-limit, max=limit).astype(held_as)


def setup_inputs(seed: int = 0) -> dict:
    key_of = jax.random.split(jax.random.key(seed), 9)
    return {
        "hidden": bell_draw(key_of[0], (NB * BT, D), 1.0, 6.0, ((0, 64), (1, 8))),
        "queries": draw_queries(jax.random.fold_in(key_of[8], 71), 0),
        "out_grad": bell_draw(key_of[2], (NB * BT, HQ * HD), 4.0, 16.0, ((0, 64), (1, 8))),
        "w_key": bell_draw(key_of[3], (D, KVH * HD), D ** -0.5, 0.078125, ((1, 8),)),
        "w_value": bell_draw(key_of[4], (D, KVH * HD), D ** -0.5, 0.078125, ((1, 8),)),
        "prompt_kv": draw_prompt_kv(jax.random.fold_in(key_of[8], 71), 0),
        "block_dest": draw_block_dest(jax.random.fold_in(key_of[8], 71), 0),
        "resp_len": draw_resp_len(jax.random.fold_in(key_of[8], 71), 0),
    }


big_negative = -1e+30

def one_block(inputs, w_key, w_value):
    block_hidden, block_query, block_upstream, prompt_pair, length = inputs
    group_size = HQ // KVH
    key_count = PL + BT
    resp_keys = jnp.dot(block_hidden, w_key, preferred_element_type=jnp.float32).astype(jnp.bfloat16)
    resp_values = jnp.dot(block_hidden, w_value, preferred_element_type=jnp.float32).astype(jnp.bfloat16)
    all_keys = jnp.concatenate([prompt_pair[0], resp_keys], axis=0)
    all_values = jnp.concatenate([prompt_pair[1], resp_values], axis=0)
    row_pos = lax.broadcasted_iota(jnp.int32, (BT, key_count), 0)
    col_pos = lax.broadcasted_iota(jnp.int32, (BT, key_count), 1) - PL
    visible = (col_pos < 0) | (col_pos <= row_pos) & (col_pos < length)
    query_full = block_query.astype(jnp.float32).reshape(BT, KVH, group_size, HD)
    keys_full = all_keys.astype(jnp.float32).reshape(key_count, KVH, HD)
    values_full = all_values.astype(jnp.float32).reshape(key_count, KVH, HD)
    live_rows = lax.broadcasted_iota(jnp.int32, (BT, 1, 1, 1), 0) < length
    upstream = jnp.where(live_rows, block_upstream.reshape(BT, KVH, group_size, HD), jnp.zeros((), jnp.bfloat16)).astype(jnp.float32)
    score_scale = 1.0 / math.sqrt(HD)
    scores = jnp.einsum('ikgd,jkd->kgij', query_full, keys_full) * score_scale
    scores = jnp.where(visible, scores, big_negative)
    row_peak = lax.optimization_barrier(jnp.max(scores, axis=3, keepdims=True))
    exponent = jnp.exp(scores - row_peak)
    softmax_out = exponent / lax.optimization_barrier(jnp.sum(exponent, axis=3, keepdims=True))
    weights = lax.optimization_barrier(softmax_out.astype(jnp.bfloat16)).astype(jnp.float32)
    attended = jnp.einsum('kgij,jkd->ikgd', weights, values_full)
    row_dot = lax.optimization_barrier(jnp.sum(upstream * attended, axis=3))
    prob_grad = jnp.einsum('ikgd,jkd->kgij', upstream, values_full)
    score_grad = softmax_out * (prob_grad - jnp.transpose(row_dot, (1, 2, 0))[..., None])
    score_grad = lax.optimization_barrier(score_grad.astype(jnp.bfloat16)).astype(jnp.float32)
    grad_query = (jnp.einsum('kgij,jkd->ikgd', score_grad, keys_full) * score_scale).astype(jnp.bfloat16)
    key_grad = jnp.einsum('kgij,ikgd->jkd', score_grad, query_full) * score_scale
    value_grad = jnp.einsum('kgij,ikgd->jkd', weights, upstream)
    key_grad = key_grad.reshape(key_count, KVH * HD)
    value_grad = value_grad.reshape(key_count, KVH * HD)
    prompt_grad = jnp.stack([key_grad[:PL], value_grad[:PL]]).astype(jnp.bfloat16)
    resp_key_grad = key_grad[PL:].astype(jnp.bfloat16)
    resp_value_grad = value_grad[PL:].astype(jnp.bfloat16)
    hidden_grad = jnp.dot(resp_key_grad, w_key.T, preferred_element_type=jnp.float32)
    hidden_grad = hidden_grad + jnp.dot(resp_value_grad, w_value.T, preferred_element_type=jnp.float32)
    return (grad_query.reshape(BT, HQ * HD), hidden_grad.astype(jnp.bfloat16), prompt_grad)

def reference(hidden, queries, out_grad, w_key, w_value, prompt_kv, block_dest, resp_len):
    nblocks = block_dest.shape[0]
    inputs = (hidden.reshape(nblocks, BT, D), queries.reshape(nblocks, BT, HQ * HD), out_grad.reshape(nblocks, BT, HQ * HD), prompt_kv[block_dest], resp_len)
    grad_query, hidden_grad, prompt_grad = lax.map(lambda block_in: one_block(block_in, w_key, w_value), inputs)
    grad_prompt = jax.ops.segment_sum(prompt_grad.astype(jnp.float32), block_dest, num_segments=nblocks)
    return (grad_query.reshape(nblocks * BT, HQ * HD), hidden_grad.reshape(nblocks * BT, D), grad_prompt.astype(jnp.bfloat16))
```

```python
import math

import jax
import jax.numpy as jnp
from jax import lax
from jax.experimental import pallas as pl
from jax.experimental.pallas import tpu as pltpu
from jax.sharding import PartitionSpec as P

HD = 128
GROUP = 4
CHUNKS = 4
MESH = pl.DeviceIdType.MESH
BF16 = jnp.bfloat16
F32 = jnp.float32


def dot_nt(a, b):
    return lax.dot_general(a, b, (((1,), (1,)), ((), ())), preferred_element_type=F32)


def dot(a, b):
    return jnp.dot(a, b, preferred_element_type=F32)


def kernel(
    dest_ref, len_ref, hidden_ref, q_ref, u_ref, wk_ref, wv_ref, kv_ref,
    gq_out, gh_out, gp_out,
    own, fwd_a, fwd_b, fwd_c, fwd_relay, ret_own, ret_a, ret_b, ret_c, ret_relay, ret_sum,
    q_rows, u_rows, keys, scores, prob_grads, weights, score_grads,
    w, hid, sib_send, sib_recv, y_send, y_recv, gq_tile, gh_tile,
    fwd_s1, fwd_s2, fwd_ra, fwd_rb, fwd_rc, ret_s1, ret_s2, ret_ra, ret_rb, ret_rc,
    hid_ys, hid_yr, hid_ss, hid_sr, gh_ss, gh_sr, gh_ys, gh_yr,
    own_sem, q_sem, u_sem, w_sem, hid_sem, out_sem, gq_sem, gh_sem,
):
    rows = q_ref.shape[0]
    heads = q_ref.shape[1] // HD
    all_rows = heads * rows
    prompt_len = kv_ref.shape[1]
    key_count = prompt_len + rows
    chunk = prompt_len // CHUNKS
    total = 2 * CHUNKS
    shard_cols = hidden_ref.shape[1]
    scale = 1.0 / math.sqrt(HD)

    me = lax.axis_index("dp")
    r = lax.rem(me, GROUP)
    base = me - r
    mate = r + 1 - 2 * lax.rem(r, 2)
    opp = GROUP - 1 - r
    far = lax.rem(r + 2, GROUP)
    is_edge = (r == 0) | (r == GROUP - 1)
    is_middle = (r == 1) | (r == GROUP - 2)
    tensor = lax.axis_index("tensor")
    core = lax.rem(tensor, 2)
    y = tensor // 2
    sibling = tensor + 1 - 2 * core

    def y_peer(step):
        return lax.rem(y + step, 4) * 2 + core

    def along_z(src, dst, send, recv, place):
        return pltpu.make_async_remote_copy(
            src_ref=src, dst_ref=dst, send_sem=send, recv_sem=recv,
            device_id={"dp": base + place}, device_id_type=MESH,
        )

    def along_t(src, dst, send, recv, place):
        return pltpu.make_async_remote_copy(
            src_ref=src, dst_ref=dst, send_sem=send, recv_sem=recv,
            device_id={"tensor": place}, device_id_type=MESH,
        )

    def own_copy(c):
        return pltpu.make_async_copy(
            kv_ref.at[c // CHUNKS, pl.ds((c % CHUNKS) * chunk, chunk)], own.at[c], own_sem.at[c]
        )

    def head_copies(h):
        span = pl.ds(h * HD, HD)
        place = pl.ds(h * rows, rows)
        return (
            pltpu.make_async_copy(q_ref.at[:, span], q_rows.at[place], q_sem.at[h]),
            pltpu.make_async_copy(u_ref.at[:, span], u_rows.at[place], u_sem.at[h]),
        )

    w_copies = (
        pltpu.make_async_copy(wk_ref, w.at[:, :, pl.ds(0, HD)], w_sem.at[0]),
        pltpu.make_async_copy(wv_ref, w.at[:, :, pl.ds(HD, HD)], w_sem.at[1]),
    )
    hid_copy = pltpu.make_async_copy(hidden_ref, hid.at[0, 0], hid_sem)

    for h in range(heads):
        for copy in head_copies(h):
            copy.start()
    for c in range(total):
        own_copy(c).start()
    hid_copy.start()
    for copy in w_copies:
        copy.start()

    barrier = pltpu.get_barrier_semaphore()
    for step in range(1, GROUP):
        pl.semaphore_signal(
            barrier, inc=1, device_id={"dp": base + lax.rem(r + step, GROUP)}, device_id_type=MESH
        )
        pl.semaphore_signal(
            barrier, inc=1, device_id={"tensor": y_peer(step)}, device_id_type=MESH
        )
    pl.semaphore_signal(barrier, inc=1, device_id={"tensor": sibling}, device_id_type=MESH)
    pl.semaphore_wait(barrier, 2 * (GROUP - 1) + 1)

    def kv_part(c):
        return kv_ref.at[c // CHUNKS, pl.ds((c % CHUNKS) * chunk, chunk)]

    def fwd_near(c):
        return along_z(kv_part(c), fwd_a.at[c], fwd_s1.at[c], fwd_ra.at[c], mate)

    def fwd_far(c):
        return along_z(kv_part(c), fwd_c.at[c], fwd_s2.at[c], fwd_rc.at[c], far)

    def fwd_opp(c):
        return along_z(kv_part(c), fwd_b.at[c], fwd_s2.at[c], fwd_rb.at[c], opp)

    def fwd_relayed(c):
        return along_z(fwd_relay.at[c], fwd_a.at[c], fwd_s1.at[c], fwd_ra.at[c], mate)

    @pl.when(is_edge)
    def _():
        for c in range(total):
            fwd_far(c).start()
            fwd_near(c).start()

    @pl.when(is_middle)
    def _():
        for c in range(total):
            fwd_opp(c).start()

    def hid_to_y(step):
        return along_t(
            hidden_ref, hid.at[4 - step, 0], hid_ys.at[step], hid_yr.at[4 - step], y_peer(step)
        )

    def hid_from_y(step):
        return along_t(hidden_ref, hid.at[step, 0], hid_ys.at[step], hid_yr.at[step], y_peer(step))

    def hid_to_sibling(step):
        src = hidden_ref if step == 0 else hid.at[step, 0]
        return along_t(src, hid.at[step, 1], hid_ss.at[step], hid_sr.at[step], sibling)

    hid_to_sibling(0).start()
    for step in (2, 1, 3):
        hid_to_y(step).start()

    dest_of = [dest_ref[base + place] - base for place in range(GROUP)]
    my_dest = dest_ref[me] - base
    mate_dest = dest_ref[base + mate] - base
    opp_dest = dest_ref[base + opp] - base
    far_dest = dest_ref[base + far] - base
    length = len_ref[me]
    use_own = my_dest == r
    use_a = is_edge | (my_dest == mate)
    use_b = my_dest == opp

    def arrive(c):
        own_copy(c).wait()
        fwd_near(c).wait_recv()

        @pl.when(is_middle)
        def _():
            fwd_opp(c).wait_recv()
            along_z(kv_part(c), fwd_c.at[c], fwd_s2.at[c], fwd_rc.at[c], far).wait_recv()
            other = jnp.where(mate_dest == opp, fwd_b[c], fwd_c[c])
            fwd_relay[c] = jnp.where(mate_dest == r, own[c], other)
            fwd_relayed(c).start()

        other = jnp.where(use_b, fwd_b[c], fwd_c[c])
        return jnp.where(use_own, own[c], jnp.where(use_a, fwd_a[c], other))

    for h in range(heads):
        for copy in head_copies(h):
            copy.wait()

    def mask_upstream(h, carry):
        place = pl.ds(h * rows, rows)
        live = lax.broadcasted_iota(jnp.int32, (rows, HD), 0) < length
        u_rows[place] = jnp.where(live, u_rows[place].astype(F32), 0.0).astype(BF16)
        return carry

    lax.fori_loop(0, heads, mask_upstream, 0)

    peak = jnp.full((1, all_rows), -jnp.inf, F32)
    for c in range(CHUNKS):
        part = arrive(c)
        span = pl.ds(c * chunk, chunk)
        keys[span] = part
        scores[span] = dot_nt(part, q_rows[...])
        peak = jnp.maximum(peak, jnp.max(scores[span], axis=0, keepdims=True))
        if c > 0:
            hid_from_y(c).wait_recv()
            hid_to_sibling(c).start()

    hid_copy.wait()
    for copy in w_copies:
        copy.wait()
    resp = jnp.zeros((rows, 2 * HD), F32)
    for step in range(4):
        resp = resp + dot(hid[step, 0], w[y_peer(step)])
    for step in range(4):
        hid_to_sibling(step).wait_recv()
        resp = resp + dot(hid[step, 1], w[lax.rem(y + step, 4) * 2 + 1 - core])
    resp = resp.astype(BF16)
    resp_keys, resp_values = resp[:, :HD], resp[:, HD:]
    tail = pl.ds(prompt_len, rows)
    keys[tail] = resp_keys
    key_pos = lax.broadcasted_iota(jnp.int32, (rows, all_rows), 0)
    row_pos = lax.rem(lax.broadcasted_iota(jnp.int32, (rows, all_rows), 1), rows)
    visible = (key_pos <= row_pos) & (key_pos < length)
    scores[tail] = jnp.where(visible, dot_nt(resp_keys, q_rows[...]), -1e30)
    peak = jnp.maximum(peak, jnp.max(scores[tail], axis=0, keepdims=True))

    factor = scale * math.log2(math.e)
    tile = 64
    tiles = key_count // tile

    def exponents(i, total_sum):
        span = pl.ds(i * tile, tile)
        value = jnp.exp2((scores[span] - peak) * factor)
        scores[span] = value
        return total_sum + jnp.sum(value.reshape(tile // 8, 8, all_rows), axis=0)

    sums = lax.fori_loop(0, tiles, exponents, jnp.zeros((8, all_rows), F32))
    inverse = 1.0 / jnp.sum(sums, axis=0, keepdims=True)

    def normalise(i, carry):
        span = pl.ds(i * tile, tile)
        value = scores[span] * inverse
        scores[span] = value
        weights[span] = value.astype(BF16)
        return carry

    lax.fori_loop(0, tiles, normalise, 0)

    def ret_near(c):
        return along_z(ret_own.at[c], ret_a.at[c], ret_s1.at[c], ret_ra.at[c], mate)

    def ret_far(c):
        return along_z(ret_own.at[c], ret_c.at[c], ret_s2.at[c], ret_rc.at[c], far)

    def ret_opp(c):
        return along_z(ret_own.at[c], ret_b.at[c], ret_s2.at[c], ret_rb.at[c], opp)

    def ret_relayed(c):
        return along_z(ret_relay.at[c], ret_a.at[c], ret_s1.at[c], ret_ra.at[c], mate)

    def send_back(c):
        @pl.when(is_edge)
        def _():
            ret_far(c).start()
            ret_near(c).start()

        @pl.when(is_middle)
        def _():
            ret_opp(c).start()

    def grads_of_values(start, count, values):
        span = pl.ds(start, count)
        grads = dot_nt(values, u_rows[...])
        prob_grads[span] = grads
        seen = grads * weights[span].astype(F32)
        return jnp.sum(seen, axis=0, keepdims=True)

    row_dot = grads_of_values(prompt_len, rows, resp_values)
    grad_value = dot(weights[tail], u_rows[...]).astype(BF16)
    for c in range(CHUNKS):
        part = arrive(CHUNKS + c)
        span = pl.ds(c * chunk, chunk)
        row_dot = row_dot + grads_of_values(c * chunk, chunk, part)
        ret_own[c] = dot(weights[span], u_rows[...]).astype(BF16)
        send_back(c)

    def grads_of_scores(i, carry):
        span = pl.ds(i * tile, tile)
        score_grads[span] = (scores[span] * (prob_grads[span] - row_dot)).astype(BF16)
        return carry

    per_chunk = chunk // tile
    for c in range(CHUNKS):
        span = pl.ds(c * chunk, chunk)
        lax.fori_loop(c * per_chunk, (c + 1) * per_chunk, grads_of_scores, 0)
        ret_own[CHUNKS + c] = (dot(score_grads[span], q_rows[...]) * scale).astype(BF16)
        send_back(CHUNKS + c)
    lax.fori_loop(CHUNKS * per_chunk, tiles, grads_of_scores, 0)
    grad_key = (dot(score_grads[tail], q_rows[...]) * scale).astype(BF16)

    resp_grads = jnp.concatenate([grad_key, grad_value], axis=1)

    def gh_to_sibling(step):
        return along_t(
            sib_send.at[step], sib_recv.at[step], gh_ss.at[step], gh_sr.at[step], sibling
        )

    def gh_to_y(step):
        return along_t(
            y_send.at[step], y_recv.at[4 - step], gh_ys.at[step], gh_yr.at[4 - step], y_peer(step)
        )

    def gh_from_y(step):
        return along_t(
            y_send.at[step], y_recv.at[step], gh_ys.at[step], gh_yr.at[step], y_peer(step)
        )

    for step in (2, 1, 3, 0):
        shard = lax.rem(y + step, 4) * 2 + 1 - core
        sib_send[step] = dot_nt(resp_grads, w[shard]).astype(BF16)
        gh_to_sibling(step).start()

    keys_t = keys[...].T
    gq_t = dot(keys_t, score_grads[...]) * scale
    for h in range(heads):
        gq_tile[:, pl.ds(h * HD, HD)] = gq_t[:, h * rows : (h + 1) * rows].T.astype(BF16)
    gq_copy = pltpu.make_async_copy(gq_tile, gq_out, gq_sem)
    gq_copy.start()

    def hidden_terms():
        for step in (2, 1, 3, 0):
            gh_to_sibling(step).wait_recv()
            term = dot_nt(resp_grads, w[y_peer(step)]) + sib_recv[step].astype(F32)
            y_send[step] = term.astype(BF16)
            if step > 0:
                gh_to_y(step).start()

    gh_copy = pltpu.make_async_copy(gh_tile, gh_out, gh_sem)

    def hidden_sum():
        summed = y_send[0].astype(F32)
        for step in (1, 3, 2):
            gh_from_y(step).wait_recv()
            summed = summed + y_recv[step].astype(F32)
        gh_tile[...] = summed.astype(BF16)
        gh_copy.start()

    def out_copy(c):
        where = gp_out.at[1 - c // CHUNKS, pl.ds((c % CHUNKS) * chunk, chunk)]
        return pltpu.make_async_copy(ret_sum.at[c], where, out_sem.at[c])

    def kept(flag, value):
        return jnp.where(flag, value.astype(F32), 0.0)

    for c in range(total):
        @pl.when(is_middle)
        def _():
            ret_opp(c).wait_recv()
            along_z(ret_own.at[c], ret_c.at[c], ret_s2.at[c], ret_rc.at[c], far).wait_recv()
            passed = (
                kept(my_dest == mate, ret_own[c])
                + kept(opp_dest == mate, ret_b[c])
                + kept(far_dest == mate, ret_c[c])
            )
            ret_relay[c] = passed.astype(BF16)
            ret_relayed(c).start()

        ret_near(c).wait_recv()
        summed = kept(my_dest == r, ret_own[c]) + kept(is_edge | (mate_dest == r), ret_a[c])
        summed = summed + kept(is_middle & (opp_dest == r), ret_b[c])
        summed = summed + kept(is_middle & (far_dest == r), ret_c[c])
        ret_sum[c] = summed.astype(BF16)
        out_copy(c).start()
        if c == 0:
            hidden_terms()
        if c == total - 2:
            hidden_sum()

    gq_copy.wait()
    gh_copy.wait()
    for step in range(4):
        hid_to_sibling(step).wait_send()
        gh_to_sibling(step).wait_send()
        if step > 0:
            hid_to_y(step).wait_send()
            gh_to_y(step).wait_send()
    for c in range(total):
        fwd_near(c).wait_send()
        fwd_opp(c).wait_send()
        ret_near(c).wait_send()
        ret_opp(c).wait_send()
        out_copy(c).wait()


def local(hidden, queries, out_grad, w_key, w_value, prompt_kv, block_dest, resp_len):
    rows, q_cols = queries.shape
    shard_cols = hidden.shape[1]
    shards = w_key.shape[0] // shard_cols
    kv_cols = w_key.shape[1]
    prompt_len = prompt_kv.shape[2]
    chunk = prompt_len // CHUNKS
    total = 2 * CHUNKS
    all_rows = q_cols // HD * rows
    heads = q_cols // HD
    key_count = prompt_len + rows
    dma = pltpu.SemaphoreType.DMA
    part = pltpu.VMEM((total, chunk, kv_cols), BF16)
    shard = (rows, shard_cols)
    any_space = pl.BlockSpec(memory_space=pl.ANY)
    smem = pl.BlockSpec(memory_space=pltpu.SMEM)
    scratch = (
        [part] * 11
        + [pltpu.VMEM((all_rows, HD), BF16)] * 2
        + [
            pltpu.VMEM((key_count, HD), BF16),
            pltpu.VMEM((key_count, all_rows), F32),
            pltpu.VMEM((key_count, all_rows), F32),
            pltpu.VMEM((key_count, all_rows), BF16),
            pltpu.VMEM((key_count, all_rows), BF16),
            pltpu.VMEM((shards, shard_cols, 2 * kv_cols), BF16),
            pltpu.VMEM((4, 2) + shard, BF16),
        ]
        + [pltpu.VMEM((4,) + shard, BF16)] * 4
        + [pltpu.VMEM((rows, q_cols), BF16), pltpu.VMEM(shard, BF16)]
        + [dma((total,))] * 10
        + [dma((4,))] * 8
        + [dma((total,)), dma((heads,)), dma((heads,)), dma((2,)), dma, dma((total,)), dma, dma]
    )
    grad_query, grad_hidden, grad_prompt = pl.pallas_call(
        kernel,
        out_shape=(
            jax.ShapeDtypeStruct(queries.shape, BF16),
            jax.ShapeDtypeStruct(hidden.shape, BF16),
            jax.ShapeDtypeStruct(prompt_kv.shape[1:], BF16),
        ),
        in_specs=[smem] * 2 + [any_space] * 6,
        out_specs=[any_space] * 3,
        scratch_shapes=scratch,
        compiler_params=pltpu.CompilerParams(
            collective_id=0, has_side_effects=True, vmem_limit_bytes=48 * 1024 * 1024
        ),
        name="attention_backward",
    )(
        block_dest, resp_len, hidden, queries, out_grad,
        w_key.reshape(shards, shard_cols, kv_cols), w_value.reshape(shards, shard_cols, kv_cols),
        prompt_kv[0],
    )
    return grad_query, grad_hidden, grad_prompt[None]


def solution(mesh):
    return jax.shard_map(
        local,
        mesh=mesh,
        in_specs=(
            P("dp", "tensor"),
            P("dp", "tensor"),
            P("dp", "tensor"),
            P(None, "tensor"),
            P(None, "tensor"),
            P("dp", None, None, "tensor"),
            P(),
            P(),
        ),
        out_specs=(P("dp", "tensor"), P("dp", "tensor"), P("dp", None, None, "tensor")),
        check_vma=False,
    )
```

```python
import math

import jax
import jax.numpy as jnp
from jax import lax
from jax.experimental import pallas as pl
from jax.experimental.pallas import tpu as pltpu
from jax.sharding import PartitionSpec as P

HD = 128
GROUP = 4
CHUNKS = 4
MESH = pl.DeviceIdType.MESH
BF16 = jnp.bfloat16
F32 = jnp.float32


def dot_nt(a, b):
    return lax.dot_general(a, b, (((1,), (1,)), ((), ())), preferred_element_type=F32)


def dot(a, b):
    return jnp.dot(a, b, preferred_element_type=F32)


def kernel(
    dest_ref, len_ref, hidden_ref, q_ref, u_ref, wk_ref, wv_ref, kv_ref,
    gq_out, gh_out, gp_out,
    own, fwd_a, fwd_b, fwd_c, fwd_relay, ret_own, ret_a, ret_b, ret_c, ret_relay, ret_sum,
    q_rows, u_rows, keys, scores, prob_grads, weights, score_grads,
    w, hid, sib_send, sib_recv, y_send, y_recv, gq_tile, gh_tile,
    fwd_s1, fwd_s2, fwd_ra, fwd_rb, fwd_rc, ret_s1, ret_s2, ret_ra, ret_rb, ret_rc,
    hid_ys, hid_yr, hid_ss, hid_sr, gh_ss, gh_sr, gh_ys, gh_yr,
    own_sem, q_sem, u_sem, w_sem, hid_sem, out_sem, gq_sem, gh_sem,
    dests, lengths, dest_sem, len_sem,
):
    rows = q_ref.shape[0]
    heads = q_ref.shape[1] // HD
    all_rows = heads * rows
    prompt_len = kv_ref.shape[1]
    key_count = prompt_len + rows
    chunk = prompt_len // CHUNKS
    total = 2 * CHUNKS
    shard_cols = hidden_ref.shape[1]
    scale = 1.0 / math.sqrt(HD)

    me = lax.axis_index("dp")
    r = lax.rem(me, GROUP)
    base = me - r
    mate = r + 1 - 2 * lax.rem(r, 2)
    opp = GROUP - 1 - r
    far = lax.rem(r + 2, GROUP)
    is_edge = (r == 0) | (r == GROUP - 1)
    is_middle = (r == 1) | (r == GROUP - 2)
    tensor = lax.axis_index("tensor")
    core = lax.rem(tensor, 2)
    y = tensor // 2
    sibling = tensor + 1 - 2 * core

    def y_peer(step):
        return lax.rem(y + step, 4) * 2 + core

    def along_z(src, dst, send, recv, place):
        return pltpu.make_async_remote_copy(
            src_ref=src, dst_ref=dst, send_sem=send, recv_sem=recv,
            device_id={"dp": base + place}, device_id_type=MESH,
        )

    def along_t(src, dst, send, recv, place):
        return pltpu.make_async_remote_copy(
            src_ref=src, dst_ref=dst, send_sem=send, recv_sem=recv,
            device_id={"tensor": place}, device_id_type=MESH,
        )

    def own_copy(c):
        return pltpu.make_async_copy(
            kv_ref.at[c // CHUNKS, pl.ds((c % CHUNKS) * chunk, chunk)], own.at[c], own_sem.at[c]
        )

    def head_copies(h):
        span = pl.ds(h * HD, HD)
        place = pl.ds(h * rows, rows)
        return (
            pltpu.make_async_copy(q_ref.at[:, span], q_rows.at[place], q_sem.at[h]),
            pltpu.make_async_copy(u_ref.at[:, span], u_rows.at[place], u_sem.at[h]),
        )

    w_copies = (
        pltpu.make_async_copy(wk_ref, w.at[:, :, pl.ds(0, HD)], w_sem.at[0]),
        pltpu.make_async_copy(wv_ref, w.at[:, :, pl.ds(HD, HD)], w_sem.at[1]),
    )
    hid_copy = pltpu.make_async_copy(hidden_ref, hid.at[0, 0], hid_sem)

    dest_copy = pltpu.make_async_copy(dest_ref, dests, dest_sem)
    len_copy = pltpu.make_async_copy(len_ref, lengths, len_sem)
    dest_copy.start()
    len_copy.start()
    for h in range(heads):
        for copy in head_copies(h):
            copy.start()
    for c in range(total):
        own_copy(c).start()
    hid_copy.start()
    for copy in w_copies:
        copy.start()

    barrier = pltpu.get_barrier_semaphore()
    for step in range(1, GROUP):
        pl.semaphore_signal(
            barrier, inc=1, device_id={"dp": base + lax.rem(r + step, GROUP)}, device_id_type=MESH
        )
        pl.semaphore_signal(
            barrier, inc=1, device_id={"tensor": y_peer(step)}, device_id_type=MESH
        )
    pl.semaphore_signal(barrier, inc=1, device_id={"tensor": sibling}, device_id_type=MESH)
    pl.semaphore_wait(barrier, 2 * (GROUP - 1) + 1)

    def kv_part(c):
        return kv_ref.at[c // CHUNKS, pl.ds((c % CHUNKS) * chunk, chunk)]

    def fwd_near(c):
        return along_z(kv_part(c), fwd_a.at[c], fwd_s1.at[c], fwd_ra.at[c], mate)

    def fwd_far(c):
        return along_z(kv_part(c), fwd_c.at[c], fwd_s2.at[c], fwd_rc.at[c], far)

    def fwd_opp(c):
        return along_z(kv_part(c), fwd_b.at[c], fwd_s2.at[c], fwd_rb.at[c], opp)

    def fwd_relayed(c):
        return along_z(fwd_relay.at[c], fwd_a.at[c], fwd_s1.at[c], fwd_ra.at[c], mate)

    @pl.when(is_edge)
    def _():
        for c in range(total):
            fwd_far(c).start()
            fwd_near(c).start()

    @pl.when(is_middle)
    def _():
        for c in range(total):
            fwd_opp(c).start()

    def hid_to_y(step):
        return along_t(
            hidden_ref, hid.at[4 - step, 0], hid_ys.at[step], hid_yr.at[4 - step], y_peer(step)
        )

    def hid_from_y(step):
        return along_t(hidden_ref, hid.at[step, 0], hid_ys.at[step], hid_yr.at[step], y_peer(step))

    def hid_to_sibling(step):
        src = hidden_ref if step == 0 else hid.at[step, 0]
        return along_t(src, hid.at[step, 1], hid_ss.at[step], hid_sr.at[step], sibling)

    hid_to_sibling(0).start()
    for step in (2, 1, 3):
        hid_to_y(step).start()

    dest_copy.wait()
    len_copy.wait()
    my_dest = dests[me] - base
    mate_dest = dests[base + mate] - base
    opp_dest = dests[base + opp] - base
    far_dest = dests[base + far] - base
    length = lengths[me]
    use_own = my_dest == r
    use_a = is_edge | (my_dest == mate)
    use_b = my_dest == opp

    def arrive(c):
        own_copy(c).wait()
        fwd_near(c).wait_recv()

        @pl.when(is_middle)
        def _():
            fwd_opp(c).wait_recv()
            along_z(kv_part(c), fwd_c.at[c], fwd_s2.at[c], fwd_rc.at[c], far).wait_recv()
            other = jnp.where(mate_dest == opp, fwd_b[c], fwd_c[c])
            fwd_relay[c] = jnp.where(mate_dest == r, own[c], other)
            fwd_relayed(c).start()

        other = jnp.where(use_b, fwd_b[c], fwd_c[c])
        return jnp.where(use_own, own[c], jnp.where(use_a, fwd_a[c], other))

    for h in range(heads):
        for copy in head_copies(h):
            copy.wait()

    def mask_upstream(h, carry):
        place = pl.ds(h * rows, rows)
        live = lax.broadcasted_iota(jnp.int32, (rows, HD), 0) < length
        u_rows[place] = jnp.where(live, u_rows[place].astype(F32), 0.0).astype(BF16)
        return carry

    lax.fori_loop(0, heads, mask_upstream, 0)

    peak = jnp.full((1, all_rows), -jnp.inf, F32)
    for c in range(CHUNKS):
        part = arrive(c)
        span = pl.ds(c * chunk, chunk)
        keys[span] = part
        scores[span] = dot_nt(part, q_rows[...])
        peak = jnp.maximum(peak, jnp.max(scores[span], axis=0, keepdims=True))
        if c > 0:
            hid_from_y(c).wait_recv()
            hid_to_sibling(c).start()

    hid_copy.wait()
    for copy in w_copies:
        copy.wait()
    resp = jnp.zeros((rows, 2 * HD), F32)
    for step in range(4):
        resp = resp + dot(hid[step, 0], w[y_peer(step)])
    for step in range(4):
        hid_to_sibling(step).wait_recv()
        resp = resp + dot(hid[step, 1], w[lax.rem(y + step, 4) * 2 + 1 - core])
    resp = resp.astype(BF16)
    resp_keys, resp_values = resp[:, :HD], resp[:, HD:]
    tail = pl.ds(prompt_len, rows)
    keys[tail] = resp_keys
    key_pos = lax.broadcasted_iota(jnp.int32, (rows, all_rows), 0)
    row_pos = lax.rem(lax.broadcasted_iota(jnp.int32, (rows, all_rows), 1), rows)
    visible = (key_pos <= row_pos) & (key_pos < length)
    scores[tail] = jnp.where(visible, dot_nt(resp_keys, q_rows[...]), -1e30)
    peak = jnp.maximum(peak, jnp.max(scores[tail], axis=0, keepdims=True))

    factor = scale * math.log2(math.e)
    tile = 64
    tiles = key_count // tile

    def exponents(i, total_sum):
        span = pl.ds(i * tile, tile)
        value = jnp.exp2((scores[span] - peak) * factor)
        scores[span] = value
        return total_sum + jnp.sum(value.reshape(tile // 8, 8, all_rows), axis=0)

    sums = lax.fori_loop(0, tiles, exponents, jnp.zeros((8, all_rows), F32))
    inverse = 1.0 / jnp.sum(sums, axis=0, keepdims=True)

    def normalise(i, carry):
        span = pl.ds(i * tile, tile)
        value = scores[span] * inverse
        scores[span] = value
        weights[span] = value.astype(BF16)
        return carry

    lax.fori_loop(0, tiles, normalise, 0)

    def ret_near(c):
        return along_z(ret_own.at[c], ret_a.at[c], ret_s1.at[c], ret_ra.at[c], mate)

    def ret_far(c):
        return along_z(ret_own.at[c], ret_c.at[c], ret_s2.at[c], ret_rc.at[c], far)

    def ret_opp(c):
        return along_z(ret_own.at[c], ret_b.at[c], ret_s2.at[c], ret_rb.at[c], opp)

    def ret_relayed(c):
        return along_z(ret_relay.at[c], ret_a.at[c], ret_s1.at[c], ret_ra.at[c], mate)

    def send_back(c):
        @pl.when(is_edge)
        def _():
            ret_far(c).start()
            ret_near(c).start()

        @pl.when(is_middle)
        def _():
            ret_opp(c).start()

    def grads_of_values(start, count, values):
        span = pl.ds(start, count)
        grads = dot_nt(values, u_rows[...])
        prob_grads[span] = grads
        seen = grads * weights[span].astype(F32)
        return jnp.sum(seen, axis=0, keepdims=True)

    row_dot = grads_of_values(prompt_len, rows, resp_values)
    grad_value = dot(weights[tail], u_rows[...]).astype(BF16)
    for c in range(CHUNKS):
        part = arrive(CHUNKS + c)
        span = pl.ds(c * chunk, chunk)
        row_dot = row_dot + grads_of_values(c * chunk, chunk, part)
        ret_own[c] = dot(weights[span], u_rows[...]).astype(BF16)
        send_back(c)

    def grads_of_scores(i, carry):
        span = pl.ds(i * tile, tile)
        score_grads[span] = (scores[span] * (prob_grads[span] - row_dot)).astype(BF16)
        return carry

    per_chunk = chunk // tile
    for c in range(CHUNKS):
        span = pl.ds(c * chunk, chunk)
        lax.fori_loop(c * per_chunk, (c + 1) * per_chunk, grads_of_scores, 0)
        ret_own[CHUNKS + c] = (dot(score_grads[span], q_rows[...]) * scale).astype(BF16)
        send_back(CHUNKS + c)
    lax.fori_loop(CHUNKS * per_chunk, tiles, grads_of_scores, 0)
    grad_key = (dot(score_grads[tail], q_rows[...]) * scale).astype(BF16)

    resp_grads = jnp.concatenate([grad_key, grad_value], axis=1)

    def gh_to_sibling(step):
        return along_t(
            sib_send.at[step], sib_recv.at[step], gh_ss.at[step], gh_sr.at[step], sibling
        )

    def gh_to_y(step):
        return along_t(
            y_send.at[step], y_recv.at[4 - step], gh_ys.at[step], gh_yr.at[4 - step], y_peer(step)
        )

    def gh_from_y(step):
        return along_t(
            y_send.at[step], y_recv.at[step], gh_ys.at[step], gh_yr.at[step], y_peer(step)
        )

    for step in (2, 1, 3, 0):
        shard = lax.rem(y + step, 4) * 2 + 1 - core
        sib_send[step] = dot_nt(resp_grads, w[shard]).astype(BF16)
        gh_to_sibling(step).start()

    keys_t = keys[...].T
    gq_t = dot(keys_t, score_grads[...]) * scale
    for h in range(heads):
        gq_tile[:, pl.ds(h * HD, HD)] = gq_t[:, h * rows : (h + 1) * rows].T.astype(BF16)
    gq_copy = pltpu.make_async_copy(gq_tile, gq_out, gq_sem)
    gq_copy.start()

    def hidden_terms():
        for step in (2, 1, 3, 0):
            gh_to_sibling(step).wait_recv()
            term = dot_nt(resp_grads, w[y_peer(step)]) + sib_recv[step].astype(F32)
            y_send[step] = term.astype(BF16)
            if step > 0:
                gh_to_y(step).start()

    gh_copy = pltpu.make_async_copy(gh_tile, gh_out, gh_sem)

    def hidden_sum():
        summed = y_send[0].astype(F32)
        for step in (1, 3, 2):
            gh_from_y(step).wait_recv()
            summed = summed + y_recv[step].astype(F32)
        gh_tile[...] = summed.astype(BF16)
        gh_copy.start()

    def out_copy(c):
        where = gp_out.at[1 - c // CHUNKS, pl.ds((c % CHUNKS) * chunk, chunk)]
        return pltpu.make_async_copy(ret_sum.at[c], where, out_sem.at[c])

    def kept(flag, value):
        return jnp.where(flag, value.astype(F32), 0.0)

    for c in range(total):
        @pl.when(is_middle)
        def _():
            ret_opp(c).wait_recv()
            along_z(ret_own.at[c], ret_c.at[c], ret_s2.at[c], ret_rc.at[c], far).wait_recv()
            passed = (
                kept(my_dest == mate, ret_own[c])
                + kept(opp_dest == mate, ret_b[c])
                + kept(far_dest == mate, ret_c[c])
            )
            ret_relay[c] = passed.astype(BF16)
            ret_relayed(c).start()

        ret_near(c).wait_recv()
        summed = kept(my_dest == r, ret_own[c]) + kept(is_edge | (mate_dest == r), ret_a[c])
        summed = summed + kept(is_middle & (opp_dest == r), ret_b[c])
        summed = summed + kept(is_middle & (far_dest == r), ret_c[c])
        ret_sum[c] = summed.astype(BF16)
        out_copy(c).start()
        if c == 0:
            hidden_terms()
        if c == total - 2:
            hidden_sum()

    gq_copy.wait()
    gh_copy.wait()
    for step in range(4):
        hid_to_sibling(step).wait_send()
        gh_to_sibling(step).wait_send()
        if step > 0:
            hid_to_y(step).wait_send()
            gh_to_y(step).wait_send()
    for c in range(total):
        fwd_near(c).wait_send()
        fwd_opp(c).wait_send()
        ret_near(c).wait_send()
        ret_opp(c).wait_send()
        out_copy(c).wait()


def local(hidden, queries, out_grad, w_key, w_value, prompt_kv, block_dest, resp_len):
    rows, q_cols = queries.shape
    shard_cols = hidden.shape[1]
    shards = w_key.shape[0] // shard_cols
    kv_cols = w_key.shape[1]
    prompt_len = prompt_kv.shape[2]
    chunk = prompt_len // CHUNKS
    total = 2 * CHUNKS
    all_rows = q_cols // HD * rows
    heads = q_cols // HD
    key_count = prompt_len + rows
    dma = pltpu.SemaphoreType.DMA
    part = pltpu.VMEM((total, chunk, kv_cols), BF16)
    shard = (rows, shard_cols)
    hbm = pl.BlockSpec(memory_space=pltpu.HBM)
    scratch = (
        [part] * 11
        + [pltpu.VMEM((all_rows, HD), BF16)] * 2
        + [
            pltpu.VMEM((key_count, HD), BF16),
            pltpu.VMEM((key_count, all_rows), F32),
            pltpu.VMEM((key_count, all_rows), F32),
            pltpu.VMEM((key_count, all_rows), BF16),
            pltpu.VMEM((key_count, all_rows), BF16),
            pltpu.VMEM((shards, shard_cols, 2 * kv_cols), BF16),
            pltpu.VMEM((4, 2) + shard, BF16),
        ]
        + [pltpu.VMEM((4,) + shard, BF16)] * 4
        + [pltpu.VMEM((rows, q_cols), BF16), pltpu.VMEM(shard, BF16)]
        + [dma((total,))] * 10
        + [dma((4,))] * 8
        + [dma((total,)), dma((heads,)), dma((heads,)), dma((2,)), dma, dma((total,)), dma, dma]
        + [pltpu.SMEM(block_dest.shape, jnp.int32), pltpu.SMEM(resp_len.shape, jnp.int32), dma, dma]
    )
    grad_query, grad_hidden, grad_prompt = pl.pallas_call(
        kernel,
        out_shape=(
            jax.ShapeDtypeStruct(queries.shape, BF16),
            jax.ShapeDtypeStruct(hidden.shape, BF16),
            jax.ShapeDtypeStruct(prompt_kv.shape[1:], BF16),
        ),
        in_specs=[hbm] * 8,
        out_specs=[hbm] * 3,
        scratch_shapes=scratch,
        compiler_params=pltpu.CompilerParams(
            collective_id=0, has_side_effects=True, vmem_limit_bytes=60 * 1024 * 1024
        ),
        name="attention_backward",
    )(
        block_dest, resp_len, hidden, queries, out_grad,
        w_key.reshape(shards, shard_cols, kv_cols), w_value.reshape(shards, shard_cols, kv_cols),
        prompt_kv[0],
    )
    return grad_query, grad_hidden, grad_prompt[None]


def solution(mesh):
    return jax.shard_map(
        local,
        mesh=mesh,
        in_specs=(
            P("dp", "tensor"),
            P("dp", "tensor"),
            P("dp", "tensor"),
            P(None, "tensor"),
            P(None, "tensor"),
            P("dp", None, None, "tensor"),
            P(),
            P(),
        ),
        out_specs=(P("dp", "tensor"), P("dp", "tensor"), P("dp", None, None, "tensor")),
        check_vma=False,
    )
```

```python
import math

import jax
import jax.numpy as jnp
from jax import lax
from jax.experimental import pallas as pl
from jax.experimental.pallas import tpu as pltpu
from jax.sharding import PartitionSpec as P

HD = 128
GROUP = 4
CHUNKS = 4
MESH = pl.DeviceIdType.MESH
BF16 = jnp.bfloat16
F32 = jnp.float32


def dot_nt(a, b):
    return lax.dot_general(a, b, (((1,), (1,)), ((), ())), preferred_element_type=F32)


def dot(a, b):
    return jnp.dot(a, b, preferred_element_type=F32)


def kernel(
    dest_ref, len_ref, hidden_ref, q_ref, u_ref, wk_ref, wv_ref, kv_ref,
    gq_out, gh_out, gp_out,
    own, fwd_a, fwd_b, fwd_c, fwd_relay, ret_own, ret_a, ret_b, ret_c, ret_relay,
    q_rows, u_rows, keys, scores, prob_grads, weights, score_grads,
    w, hid, sib_send, sib_recv, y_send, y_recv,
    fwd_s1, fwd_s2, fwd_ra, fwd_rb, fwd_rc, ret_s1, ret_s2, ret_ra, ret_rb, ret_rc,
    hid_ys, hid_yr, hid_ss, hid_sr, gh_ss, gh_sr, gh_ys, gh_yr,
    own_sem, q_sem, u_sem, w_sem, hid_sem,
    dests, lengths, dest_sem, len_sem,
):
    rows = q_ref.shape[0]
    heads = q_ref.shape[1] // HD
    all_rows = heads * rows
    prompt_len = kv_ref.shape[1]
    key_count = prompt_len + rows
    chunk = prompt_len // CHUNKS
    total = 2 * CHUNKS
    shard_cols = hidden_ref.shape[1]
    scale = 1.0 / math.sqrt(HD)

    me = lax.axis_index("dp")
    r = lax.rem(me, GROUP)
    base = me - r
    mate = r + 1 - 2 * lax.rem(r, 2)
    opp = GROUP - 1 - r
    far = lax.rem(r + 2, GROUP)
    is_edge = (r == 0) | (r == GROUP - 1)
    is_middle = (r == 1) | (r == GROUP - 2)
    tensor = lax.axis_index("tensor")
    core = lax.rem(tensor, 2)
    y = tensor // 2
    sibling = tensor + 1 - 2 * core

    def y_peer(step):
        return lax.rem(y + step, 4) * 2 + core

    def along_z(src, dst, send, recv, place):
        return pltpu.make_async_remote_copy(
            src_ref=src, dst_ref=dst, send_sem=send, recv_sem=recv,
            device_id={"dp": base + place}, device_id_type=MESH,
        )

    def along_t(src, dst, send, recv, place):
        return pltpu.make_async_remote_copy(
            src_ref=src, dst_ref=dst, send_sem=send, recv_sem=recv,
            device_id={"tensor": place}, device_id_type=MESH,
        )

    def own_copy(c):
        return pltpu.make_async_copy(
            kv_ref.at[c // CHUNKS, pl.ds((c % CHUNKS) * chunk, chunk)], own.at[c], own_sem.at[c]
        )

    def head_copies(h):
        span = pl.ds(h * HD, HD)
        place = pl.ds(h * rows, rows)
        return (
            pltpu.make_async_copy(q_ref.at[:, span], q_rows.at[place], q_sem.at[h]),
            pltpu.make_async_copy(u_ref.at[:, span], u_rows.at[place], u_sem.at[h]),
        )

    w_copies = (
        pltpu.make_async_copy(wk_ref, w.at[:, :, pl.ds(0, HD)], w_sem.at[0]),
        pltpu.make_async_copy(wv_ref, w.at[:, :, pl.ds(HD, HD)], w_sem.at[1]),
    )
    hid_copy = pltpu.make_async_copy(hidden_ref, hid.at[0, 0], hid_sem)

    dest_copy = pltpu.make_async_copy(dest_ref, dests, dest_sem)
    len_copy = pltpu.make_async_copy(len_ref, lengths, len_sem)
    dest_copy.start()
    len_copy.start()
    for h in range(heads):
        for copy in head_copies(h):
            copy.start()
    for c in range(total):
        own_copy(c).start()
    hid_copy.start()
    for copy in w_copies:
        copy.start()

    barrier = pltpu.get_barrier_semaphore()
    for step in range(1, GROUP):
        pl.semaphore_signal(
            barrier, inc=1, device_id={"dp": base + lax.rem(r + step, GROUP)}, device_id_type=MESH
        )
        pl.semaphore_signal(
            barrier, inc=1, device_id={"tensor": y_peer(step)}, device_id_type=MESH
        )
    pl.semaphore_signal(barrier, inc=1, device_id={"tensor": sibling}, device_id_type=MESH)
    pl.semaphore_wait(barrier, 2 * (GROUP - 1) + 1)

    def kv_part(c):
        return kv_ref.at[c // CHUNKS, pl.ds((c % CHUNKS) * chunk, chunk)]

    def fwd_near(c):
        return along_z(kv_part(c), fwd_a.at[c], fwd_s1.at[c], fwd_ra.at[c], mate)

    def fwd_far(c):
        return along_z(kv_part(c), fwd_c.at[c], fwd_s2.at[c], fwd_rc.at[c], far)

    def fwd_opp(c):
        return along_z(kv_part(c), fwd_b.at[c], fwd_s2.at[c], fwd_rb.at[c], opp)

    def fwd_relayed(c):
        return along_z(fwd_relay.at[c], fwd_a.at[c], fwd_s1.at[c], fwd_ra.at[c], mate)

    @pl.when(is_edge)
    def _():
        for c in range(total):
            fwd_far(c).start()
            fwd_near(c).start()

    @pl.when(is_middle)
    def _():
        for c in range(total):
            fwd_opp(c).start()

    def hid_to_y(step):
        return along_t(
            hidden_ref, hid.at[4 - step, 0], hid_ys.at[step], hid_yr.at[4 - step], y_peer(step)
        )

    def hid_from_y(step):
        return along_t(hidden_ref, hid.at[step, 0], hid_ys.at[step], hid_yr.at[step], y_peer(step))

    def hid_to_sibling(step):
        src = hidden_ref if step == 0 else hid.at[step, 0]
        return along_t(src, hid.at[step, 1], hid_ss.at[step], hid_sr.at[step], sibling)

    hid_to_sibling(0).start()
    for step in (2, 1, 3):
        hid_to_y(step).start()

    dest_copy.wait()
    len_copy.wait()
    my_dest = dests[me] - base
    mate_dest = dests[base + mate] - base
    opp_dest = dests[base + opp] - base
    far_dest = dests[base + far] - base
    length = lengths[me]
    use_own = my_dest == r
    use_a = is_edge | (my_dest == mate)
    use_b = my_dest == opp

    def arrive(c):
        own_copy(c).wait()
        fwd_near(c).wait_recv()

        @pl.when(is_middle)
        def _():
            fwd_opp(c).wait_recv()
            along_z(kv_part(c), fwd_c.at[c], fwd_s2.at[c], fwd_rc.at[c], far).wait_recv()
            other = jnp.where(mate_dest == opp, fwd_b[c], fwd_c[c])
            fwd_relay[c] = jnp.where(mate_dest == r, own[c], other)
            fwd_relayed(c).start()

        other = jnp.where(use_b, fwd_b[c], fwd_c[c])
        return jnp.where(use_own, own[c], jnp.where(use_a, fwd_a[c], other))

    for h in range(heads):
        for copy in head_copies(h):
            copy.wait()

    def mask_upstream(h, carry):
        place = pl.ds(h * rows, rows)
        live = lax.broadcasted_iota(jnp.int32, (rows, HD), 0) < length
        u_rows[place] = jnp.where(live, u_rows[place].astype(F32), 0.0).astype(BF16)
        return carry

    lax.fori_loop(0, heads, mask_upstream, 0)

    peak = jnp.full((1, all_rows), -jnp.inf, F32)
    for c in range(CHUNKS):
        part = arrive(c)
        span = pl.ds(c * chunk, chunk)
        keys[span] = part
        scores[span] = dot_nt(part, q_rows[...])
        peak = jnp.maximum(peak, jnp.max(scores[span], axis=0, keepdims=True))
        if c > 0:
            hid_from_y(c).wait_recv()
            hid_to_sibling(c).start()

    hid_copy.wait()
    for copy in w_copies:
        copy.wait()
    resp = jnp.zeros((rows, 2 * HD), F32)
    for step in range(4):
        resp = resp + dot(hid[step, 0], w[y_peer(step)])
    for step in range(4):
        hid_to_sibling(step).wait_recv()
        resp = resp + dot(hid[step, 1], w[lax.rem(y + step, 4) * 2 + 1 - core])
    resp = resp.astype(BF16)
    resp_keys, resp_values = resp[:, :HD], resp[:, HD:]
    tail = pl.ds(prompt_len, rows)
    keys[tail] = resp_keys
    key_pos = lax.broadcasted_iota(jnp.int32, (rows, all_rows), 0)
    row_pos = lax.rem(lax.broadcasted_iota(jnp.int32, (rows, all_rows), 1), rows)
    visible = (key_pos <= row_pos) & (key_pos < length)
    scores[tail] = jnp.where(visible, dot_nt(resp_keys, q_rows[...]), -1e30)
    peak = jnp.maximum(peak, jnp.max(scores[tail], axis=0, keepdims=True))

    factor = scale * math.log2(math.e)
    tile = 64
    tiles = key_count // tile

    def exponents(i, total_sum):
        span = pl.ds(i * tile, tile)
        value = jnp.exp2((scores[span] - peak) * factor)
        scores[span] = value
        return total_sum + jnp.sum(value.reshape(tile // 8, 8, all_rows), axis=0)

    sums = lax.fori_loop(0, tiles, exponents, jnp.zeros((8, all_rows), F32))
    inverse = 1.0 / jnp.sum(sums, axis=0, keepdims=True)

    def normalise(i, carry):
        span = pl.ds(i * tile, tile)
        value = scores[span] * inverse
        scores[span] = value
        weights[span] = value.astype(BF16)
        return carry

    lax.fori_loop(0, tiles, normalise, 0)

    def ret_near(c):
        return along_z(ret_own.at[c], ret_a.at[c], ret_s1.at[c], ret_ra.at[c], mate)

    def ret_far(c):
        return along_z(ret_own.at[c], ret_c.at[c], ret_s2.at[c], ret_rc.at[c], far)

    def ret_opp(c):
        return along_z(ret_own.at[c], ret_b.at[c], ret_s2.at[c], ret_rb.at[c], opp)

    def ret_relayed(c):
        return along_z(ret_relay.at[c], ret_a.at[c], ret_s1.at[c], ret_ra.at[c], mate)

    def send_back(c):
        @pl.when(is_edge)
        def _():
            ret_far(c).start()
            ret_near(c).start()

        @pl.when(is_middle)
        def _():
            ret_opp(c).start()

    def grads_of_values(start, count, values):
        span = pl.ds(start, count)
        grads = dot_nt(values, u_rows[...])
        prob_grads[span] = grads
        seen = grads * weights[span].astype(F32)
        return jnp.sum(seen, axis=0, keepdims=True)

    row_dot = grads_of_values(prompt_len, rows, resp_values)
    grad_value = dot(weights[tail], u_rows[...]).astype(BF16)
    for c in range(CHUNKS):
        part = arrive(CHUNKS + c)
        span = pl.ds(c * chunk, chunk)
        row_dot = row_dot + grads_of_values(c * chunk, chunk, part)
        ret_own[c] = dot(weights[span], u_rows[...]).astype(BF16)
        send_back(c)

    def grads_of_scores(i, carry):
        span = pl.ds(i * tile, tile)
        score_grads[span] = (scores[span] * (prob_grads[span] - row_dot)).astype(BF16)
        return carry

    per_chunk = chunk // tile
    for c in range(CHUNKS):
        span = pl.ds(c * chunk, chunk)
        lax.fori_loop(c * per_chunk, (c + 1) * per_chunk, grads_of_scores, 0)
        ret_own[CHUNKS + c] = (dot(score_grads[span], q_rows[...]) * scale).astype(BF16)
        send_back(CHUNKS + c)
    lax.fori_loop(CHUNKS * per_chunk, tiles, grads_of_scores, 0)
    grad_key = (dot(score_grads[tail], q_rows[...]) * scale).astype(BF16)

    resp_grads = jnp.concatenate([grad_key, grad_value], axis=1)

    def gh_to_sibling(step):
        return along_t(
            sib_send.at[step], sib_recv.at[step], gh_ss.at[step], gh_sr.at[step], sibling
        )

    def gh_to_y(step):
        return along_t(
            y_send.at[step], y_recv.at[4 - step], gh_ys.at[step], gh_yr.at[4 - step], y_peer(step)
        )

    def gh_from_y(step):
        return along_t(
            y_send.at[step], y_recv.at[step], gh_ys.at[step], gh_yr.at[step], y_peer(step)
        )

    for step in (2, 1, 3, 0):
        shard = lax.rem(y + step, 4) * 2 + 1 - core
        sib_send[step] = dot_nt(resp_grads, w[shard]).astype(BF16)
        gh_to_sibling(step).start()

    keys_t = keys[...].T
    gq_t = dot(keys_t, score_grads[...]) * scale
    for h in range(heads):
        gq_out[:, pl.ds(h * HD, HD)] = gq_t[:, h * rows : (h + 1) * rows].T.astype(BF16)

    def hidden_terms():
        for step in (2, 1, 3, 0):
            gh_to_sibling(step).wait_recv()
            term = dot_nt(resp_grads, w[y_peer(step)]) + sib_recv[step].astype(F32)
            y_send[step] = term.astype(BF16)
            if step > 0:
                gh_to_y(step).start()

    def hidden_sum():
        summed = y_send[0].astype(F32)
        for step in (1, 3, 2):
            gh_from_y(step).wait_recv()
            summed = summed + y_recv[step].astype(F32)
        gh_out[...] = summed.astype(BF16)

    def kept(flag, value):
        return jnp.where(flag, value.astype(F32), 0.0)

    for c in range(total):
        @pl.when(is_middle)
        def _():
            ret_opp(c).wait_recv()
            along_z(ret_own.at[c], ret_c.at[c], ret_s2.at[c], ret_rc.at[c], far).wait_recv()
            passed = (
                kept(my_dest == mate, ret_own[c])
                + kept(opp_dest == mate, ret_b[c])
                + kept(far_dest == mate, ret_c[c])
            )
            ret_relay[c] = passed.astype(BF16)
            ret_relayed(c).start()

        ret_near(c).wait_recv()
        summed = kept(my_dest == r, ret_own[c]) + kept(is_edge | (mate_dest == r), ret_a[c])
        summed = summed + kept(is_middle & (opp_dest == r), ret_b[c])
        summed = summed + kept(is_middle & (far_dest == r), ret_c[c])
        gp_out[1 - c // CHUNKS, pl.ds((c % CHUNKS) * chunk, chunk)] = summed.astype(BF16)
        if c == 0:
            hidden_terms()
        if c == total - 2:
            hidden_sum()

    for step in range(4):
        hid_to_sibling(step).wait_send()
        gh_to_sibling(step).wait_send()
        if step > 0:
            hid_to_y(step).wait_send()
            gh_to_y(step).wait_send()
    for c in range(total):
        fwd_near(c).wait_send()
        fwd_opp(c).wait_send()
        ret_near(c).wait_send()
        ret_opp(c).wait_send()


def write_kernel(a_ref, b_ref, c_ref, a_out, b_out, c_out, sems):
    copies = [
        pltpu.make_async_copy(src, dst, sems.at[i])
        for i, (src, dst) in enumerate(((c_ref, c_out), (a_ref, a_out), (b_ref, b_out)))
    ]
    for copy in copies:
        copy.start()
    for copy in copies:
        copy.wait()


def write_out(*arrays):
    anywhere = pl.BlockSpec(memory_space=pl.ANY)
    return pl.pallas_call(
        write_kernel,
        out_shape=tuple(jax.ShapeDtypeStruct(a.shape, a.dtype) for a in arrays),
        in_specs=[anywhere] * 3,
        out_specs=[anywhere] * 3,
        scratch_shapes=[pltpu.SemaphoreType.DMA((3,))],
        compiler_params=pltpu.CompilerParams(vmem_limit_bytes=1024 * 1024),
        name="write_out",
    )(*arrays)


def local(hidden, queries, out_grad, w_key, w_value, prompt_kv, block_dest, resp_len):
    rows, q_cols = queries.shape
    shard_cols = hidden.shape[1]
    shards = w_key.shape[0] // shard_cols
    kv_cols = w_key.shape[1]
    prompt_len = prompt_kv.shape[2]
    chunk = prompt_len // CHUNKS
    total = 2 * CHUNKS
    all_rows = q_cols // HD * rows
    heads = q_cols // HD
    key_count = prompt_len + rows
    dma = pltpu.SemaphoreType.DMA
    part = pltpu.VMEM((total, chunk, kv_cols), BF16)
    shard = (rows, shard_cols)
    hbm = pl.BlockSpec(memory_space=pltpu.HBM)
    scratch = (
        [part] * 10
        + [pltpu.VMEM((all_rows, HD), BF16)] * 2
        + [
            pltpu.VMEM((key_count, HD), BF16),
            pltpu.VMEM((key_count, all_rows), F32),
            pltpu.VMEM((key_count, all_rows), F32),
            pltpu.VMEM((key_count, all_rows), BF16),
            pltpu.VMEM((key_count, all_rows), BF16),
            pltpu.VMEM((shards, shard_cols, 2 * kv_cols), BF16),
            pltpu.VMEM((4, 2) + shard, BF16),
        ]
        + [pltpu.VMEM((4,) + shard, BF16)] * 4
        + [dma((total,))] * 10
        + [dma((4,))] * 8
        + [dma((total,)), dma((heads,)), dma((heads,)), dma((2,)), dma]
        + [pltpu.SMEM(block_dest.shape, jnp.int32), pltpu.SMEM(resp_len.shape, jnp.int32), dma, dma]
    )
    grad_query, grad_hidden, grad_prompt = pl.pallas_call(
        kernel,
        out_shape=(
            pltpu.VMEM(queries.shape, BF16),
            pltpu.VMEM(hidden.shape, BF16),
            pltpu.VMEM(prompt_kv.shape[1:], BF16),
        ),
        in_specs=[hbm] * 8,
        out_specs=[pl.BlockSpec(memory_space=pltpu.VMEM)] * 3,
        scratch_shapes=scratch,
        compiler_params=pltpu.CompilerParams(
            collective_id=0, has_side_effects=True, vmem_limit_bytes=60 * 1024 * 1024
        ),
        name="attention_backward",
    )(
        block_dest, resp_len, hidden, queries, out_grad,
        w_key.reshape(shards, shard_cols, kv_cols), w_value.reshape(shards, shard_cols, kv_cols),
        prompt_kv[0],
    )
    return write_out(grad_query, grad_hidden, grad_prompt[None])


def solution(mesh):
    return jax.shard_map(
        local,
        mesh=mesh,
        in_specs=(
            P("dp", "tensor"),
            P("dp", "tensor"),
            P("dp", "tensor"),
            P(None, "tensor"),
            P(None, "tensor"),
            P("dp", None, None, "tensor"),
            P(),
            P(),
        ),
        out_specs=(P("dp", "tensor"), P("dp", "tensor"), P("dp", None, None, "tensor")),
        check_vma=False,
    )
```

```python
import math

import jax
import jax.numpy as jnp
from jax import lax
from jax.experimental import pallas as pl
from jax.experimental.pallas import tpu as pltpu
from jax.sharding import PartitionSpec as P

HD = 128
GROUP = 4
CHUNKS = 4
MESH = pl.DeviceIdType.MESH
BF16 = jnp.bfloat16
F32 = jnp.float32


def dot_nt(a, b):
    return lax.dot_general(a, b, (((1,), (1,)), ((), ())), preferred_element_type=F32)


def dot(a, b):
    return jnp.dot(a, b, preferred_element_type=F32)


def kernel(
    dest_ref, len_ref, hidden_ref, q_ref, u_ref, wk_ref, wv_ref, kv_ref,
    gq_out, gh_out, gp_out,
    own, edge_kv, pass_kv, pass_in, relay_kv, relay_in, pg_own, pg_guest, pg_edge, pg_far, pg_relay, pg_back,
    q_rows, u_rows, guest_q, guest_u, gq_own, gq_guest, gq_back,
    keys, guest_keys, scores, guest_scores, prob_grads, weights, score_grads, resp_kv, resp_queries, resp_scores, resp_prob_grads, resp_score_grads, resp_grads,
    stat_resp, stat_guest, fin_own, fin_guest, fin_back, local_own, local_guest,
    w, hid, sib_send, sib_recv, y_send, y_recv, y_half,
    kv_s, kv_r, q_s, q_r, pass_s, pass_r, relay_s, relay_r, pe_s, pe_r, far_s, far_r, back_s, back_r,
    res_s, res_r, stat_s, stat_r, hid_ys, hid_yr, hid_ss, hid_sr, gh_ss, gh_sr, gh_ys, gh_yr,
    own_sem, qu_sem, w_sem, hid_sem, dests, lengths, small_sem,
):
    rows = q_ref.shape[0]
    heads = q_ref.shape[1] // HD
    all_rows = heads * rows
    prompt_len = kv_ref.shape[1]
    chunk = prompt_len // CHUNKS
    total = 2 * CHUNKS
    scale = 1.0 / math.sqrt(HD)
    factor = scale * math.log2(math.e)
    tile = 64

    me = lax.axis_index("dp")
    r = lax.rem(me, GROUP)
    base = me - r
    mate = r + 1 - 2 * lax.rem(r, 2)
    opp = GROUP - 1 - r
    far = lax.rem(r + 2, GROUP)
    is_edge = (r == 0) | (r == GROUP - 1)
    is_middle = (r == 1) | (r == GROUP - 2)
    tensor = lax.axis_index("tensor")
    core = lax.rem(tensor, 2)
    y = tensor // 2
    sibling = tensor + 1 - 2 * core

    def y_peer(step):
        return lax.rem(y + step, 4) * 2 + core

    def along_z(src, dst, send, recv, place):
        return pltpu.make_async_remote_copy(
            src_ref=src, dst_ref=dst, send_sem=send, recv_sem=recv,
            device_id={"dp": base + place}, device_id_type=MESH,
        )

    def along_t(src, dst, send, recv, place):
        return pltpu.make_async_remote_copy(
            src_ref=src, dst_ref=dst, send_sem=send, recv_sem=recv,
            device_id={"tensor": place}, device_id_type=MESH,
        )

    def kv_part(c):
        return kv_ref.at[c // CHUNKS, pl.ds((c % CHUNKS) * chunk, chunk)]

    def own_copy(c):
        return pltpu.make_async_copy(kv_part(c), own.at[c], own_sem.at[c])

    def head_copies(h):
        span = pl.ds(h * HD, HD)
        place = pl.ds(h * rows, rows)
        return (
            pltpu.make_async_copy(q_ref.at[:, span], q_rows.at[place], qu_sem.at[h]),
            pltpu.make_async_copy(u_ref.at[:, span], u_rows.at[place], qu_sem.at[heads + h]),
        )

    w_copies = (
        pltpu.make_async_copy(wk_ref, w.at[:, :, pl.ds(0, HD)], w_sem.at[0]),
        pltpu.make_async_copy(wv_ref, w.at[:, :, pl.ds(HD, HD)], w_sem.at[1]),
    )
    hid_copy = pltpu.make_async_copy(hidden_ref, hid.at[0, 0], hid_sem)
    dest_copy = pltpu.make_async_copy(dest_ref, dests, small_sem.at[0])
    len_copy = pltpu.make_async_copy(len_ref, lengths, small_sem.at[1])

    dest_copy.start()
    len_copy.start()
    for h in range(heads):
        for copy in head_copies(h):
            copy.start()
    for c in range(total):
        own_copy(c).start()
    hid_copy.start()
    for copy in w_copies:
        copy.start()

    barrier = pltpu.get_barrier_semaphore()
    for step in range(1, GROUP):
        pl.semaphore_signal(
            barrier, inc=1, device_id={"dp": base + lax.rem(r + step, GROUP)}, device_id_type=MESH
        )
        pl.semaphore_signal(
            barrier, inc=1, device_id={"tensor": y_peer(step)}, device_id_type=MESH
        )
    pl.semaphore_signal(barrier, inc=1, device_id={"tensor": sibling}, device_id_type=MESH)

    dest_copy.wait()
    len_copy.wait()
    my_dest = dests[me] - base
    mate_dest = dests[base + mate] - base
    opp_dest = dests[base + opp] - base
    far_dest = dests[base + far] - base
    length = lengths[me]
    in_half = is_edge | (my_dest == r) | (my_dest == mate)

    for h in range(heads):
        for copy in head_copies(h):
            copy.wait()

    def mask_upstream(h, carry):
        place = pl.ds(h * rows, rows)
        live = lax.broadcasted_iota(jnp.int32, (rows, HD), 0) < length
        u_rows[place] = jnp.where(live, u_rows[place].astype(F32), 0.0).astype(BF16)
        return carry

    lax.fori_loop(0, heads, mask_upstream, 0)
    pl.semaphore_wait(barrier, 2 * (GROUP - 1) + 1)

    def edge_send(c):
        return along_z(own.at[c], edge_kv.at[c], kv_s.at[c], kv_r.at[c], mate)

    def row_part(c):
        return pl.ds(c * (all_rows // CHUNKS), all_rows // CHUNKS)

    def query_send(c):
        src, dst = (q_rows, guest_q) if c < CHUNKS else (u_rows, guest_u)
        place = row_part(c % CHUNKS)
        return along_z(src.at[place], dst.at[place], q_s.at[c], q_r.at[c], opp)

    def pass_send(c):
        return along_z(pass_kv.at[c], pass_in.at[c], pass_s.at[c], pass_r.at[c], opp)

    def relay_send(c):
        return along_z(relay_kv.at[c], relay_in.at[c], relay_s.at[c], relay_r.at[c], mate)

    def stat_send():
        return along_z(stat_resp, stat_guest, stat_s.at[0], stat_r.at[0], opp)

    def fin_send():
        return along_z(fin_guest, fin_back, stat_s.at[1], stat_r.at[1], opp)

    def result_send(c):
        place = row_part(c)
        return along_z(gq_guest.at[place], gq_back.at[place], res_s.at[c], res_r.at[c], opp)

    def pg_edge_send(c):
        return along_z(pg_own.at[c], pg_edge.at[c], pe_s.at[c], pe_r.at[c], mate)

    def pg_far_send(c):
        return along_z(pg_edge.at[c], pg_far.at[c], far_s.at[c], far_r.at[c], opp)

    def pg_back_send(c):
        return along_z(pg_relay.at[c], pg_back.at[c], back_s.at[c], back_r.at[c], mate)

    @pl.when(is_edge)
    def _():
        for c in range(total):
            own_copy(c).wait()
            edge_send(c).start()

    @pl.when(is_middle)
    def _():
        for c in range(2):
            query_send(c).start()
        for c in range(total):
            own_copy(c).wait()

    half = rows // 2

    def hid_to_y(step):
        return along_t(
            hidden_ref, hid.at[4 - step, 0], hid_ys.at[step], hid_yr.at[4 - step], y_peer(step)
        )

    def hid_from_y(step):
        return along_t(hidden_ref, hid.at[step, 0], hid_ys.at[step], hid_yr.at[step], y_peer(step))

    def hid_onward(step):
        place = pl.ds(0 if step == 3 else half, half)
        slot = 0 if step == 3 else 2
        return along_t(
            hid.at[step, 0, place], hid.at[2, 0, place], hid_ys.at[slot], hid_yr.at[slot], y_peer(4 - step)
        )

    def hid_to_sibling(step):
        src = hidden_ref if step == 0 else hid.at[step, 0]
        return along_t(src, hid.at[step, 1], hid_ss.at[step], hid_sr.at[step], sibling)

    for step in (1, 3):
        hid_to_y(step).start()
    hid_to_sibling(0).start()

    def attend_scores(q, key_part, chunks, scores, keys, local):
        for c in chunks:
            part = key_part(c)
            span = pl.ds(c * chunk, chunk)
            keys[span] = part
            scores[span] = dot_nt(part, q[...])
            peak = jnp.max(scores[span], axis=0, keepdims=True)
            local[0:1] = peak if c == 0 else jnp.maximum(local[0:1], peak)

    def attend_exponents(scores, local):
        peak = local[0:1]

        def exponents(i, total_sum):
            span = pl.ds(i * tile, tile)
            value = jnp.exp2((scores[span] - peak) * factor)
            scores[span] = value
            return total_sum + jnp.sum(value.reshape(tile // 8, 8, all_rows), axis=0)

        sums = lax.fori_loop(0, prompt_len // tile, exponents, jnp.zeros((8, all_rows), F32))
        local[1:2] = jnp.sum(sums, axis=0, keepdims=True)

    def attend_values(u, scores, local, stats, pg, after_values, between):
        peak = jnp.maximum(local[0:1], stats[0:1])
        fade = jnp.exp2((local[0:1] - peak) * factor)
        resp_fade = jnp.exp2((stats[0:1] - peak) * factor)
        inverse = 1.0 / (local[1:2] * fade + stats[1:2] * resp_fade)
        share = fade * inverse

        def normalise(i, carry):
            span = pl.ds(i * tile, tile)
            value = scores[span] * share
            scores[span] = value
            weights[span] = value.astype(BF16)
            return carry

        lax.fori_loop(0, prompt_len // tile, normalise, 0)
        between()
        local[2:3] = peak
        local[3:4] = inverse
        local[4:5] = stats[2:3] * resp_fade * inverse
        for c in range(CHUNKS):
            pg[c] = dot(weights[pl.ds(c * chunk, chunk)], u[...]).astype(BF16)
            after_values(c)

    def attend_dot(u, value_part, local, fin):
        row_dot = local[4:5]
        for c in range(CHUNKS):
            span = pl.ds(c * chunk, chunk)
            grads = dot_nt(value_part(c), u[...])
            prob_grads[span] = grads
            seen = grads * weights[span].astype(F32)
            row_dot = row_dot + jnp.sum(seen, axis=0, keepdims=True)
        fin[0:1] = local[2:3]
        fin[1:2] = local[3:4]
        fin[2:3] = row_dot

    def attend_keys(q, scores, keys, fin, pg, gq, after_keys, before_queries=lambda: None):
        row_dot = fin[2:3]

        def grads_of_scores(i, carry):
            span = pl.ds(i * tile, tile)
            score_grads[span] = (scores[span] * (prob_grads[span] - row_dot)).astype(BF16)
            return carry

        per_chunk = chunk // tile
        for c in range(CHUNKS):
            lax.fori_loop(c * per_chunk, (c + 1) * per_chunk, grads_of_scores, 0)
            part = dot(score_grads[pl.ds(c * chunk, chunk)], q[...]) * scale
            pg[CHUNKS + c] = part.astype(BF16)
            after_keys(c)
        before_queries()
        gq_t = dot(keys[...].T, score_grads[...]) * scale
        for h in range(heads):
            gq[pl.ds(h * rows, rows)] = gq_t[:, h * rows : (h + 1) * rows].T.astype(BF16)

    def nothing(*args):
        pass

    def middle_part(c):
        return jnp.where(my_dest == r, own[c], edge_kv[c])

    def guest_part(c):
        return jnp.where(opp_dest == r, own[c], edge_kv[c])

    def edge_part(c):
        relay_send(c).wait_recv()
        return jnp.where(my_dest == r, own[c], relay_in[c])

    def pass_on(*chunks):
        for c in chunks:
            edge_send(c).wait_recv()
            pass_kv[c] = jnp.where(far_dest == r, own[c], edge_kv[c])
            pass_send(c).start()

    def pump(*chunks):
        for c in chunks:
            pass_send(c).wait_recv()
            relay_kv[c] = jnp.where(mate_dest == r, own[c], pass_in[c])
            relay_send(c).start()

    def forward(*chunks):
        for c in chunks:
            pg_edge_send(c).wait_recv()
            pg_far_send(c).start()

    @pl.when(is_middle)
    def _():
        pass_on(0, 1)
        attend_scores(q_rows, middle_part, (0, 1), scores, keys, local_own)

    hid_copy.wait()
    for copy in w_copies:
        copy.wait()
    for step in (1, 3):
        hid_from_y(step).wait_recv()
        hid_onward(step).start()
        hid_to_sibling(step).start()

    @pl.when(is_middle)
    def _():
        pump(0)
        pass_on(2, 3)
        for c in range(2, CHUNKS):
            query_send(c).start()
        attend_scores(q_rows, middle_part, (2, 3), scores, keys, local_own)
        pump(1)

    resp = dot(hid[0, 0], w[y_peer(0)])
    for step in (1, 3):
        resp = resp + dot(hid[step, 0], w[y_peer(step)])
    for slot in (0, 2):
        place = pl.ds(slot // 2 * half, half)
        along_t(
            hid.at[3 - slot, 0, place], hid.at[2, 0, place], hid_ys.at[slot], hid_yr.at[slot], sibling
        ).wait_recv()
    hid_to_sibling(2).start()

    @pl.when(is_middle)
    def _():
        pump(2)
        pass_on(4, 5)

    resp = resp + dot(hid[2, 0], w[y_peer(2)])
    for step in (0, 1, 3, 2):
        hid_to_sibling(step).wait_recv()
        resp = resp + dot(hid[step, 1], w[lax.rem(y + step, 4) * 2 + 1 - core])
    resp_kv[...] = resp.astype(BF16)

    @pl.when(is_middle)
    def _():
        pump(3)

    key_pos = lax.broadcasted_iota(jnp.int32, (rows, all_rows), 0)
    row_pos = lax.rem(lax.broadcasted_iota(jnp.int32, (rows, all_rows), 1), rows)
    visible = (key_pos <= row_pos) & (key_pos < length)
    resp_scores[...] = jnp.where(visible, dot_nt(resp_kv[:, :HD], q_rows[...]), -1e30)
    resp_prob_grads[...] = dot_nt(resp_kv[:, HD:], u_rows[...])
    resp_peak = jnp.max(resp_scores[...], axis=0, keepdims=True)
    resp_exp = jnp.exp2((resp_scores[...] - resp_peak) * factor)
    stat_resp[0:1] = resp_peak
    stat_resp[1:2] = jnp.sum(resp_exp, axis=0, keepdims=True)
    stat_resp[2:3] = jnp.sum(resp_exp * resp_prob_grads[...], axis=0, keepdims=True)

    def gh_to_sibling(step):
        return along_t(
            sib_send.at[step], sib_recv.at[step], gh_ss.at[step], gh_sr.at[step], sibling
        )

    def gh_to_y(step):
        return along_t(
            y_send.at[step], y_recv.at[4 - step], gh_ys.at[step], gh_yr.at[4 - step], y_peer(step)
        )

    def gh_from_y(step):
        return along_t(
            y_send.at[step], y_recv.at[step], gh_ys.at[step], gh_yr.at[step], y_peer(step)
        )

    def gh_half(step):
        place = pl.ds(0 if step == 1 else half, half)
        slot = 0 if step == 1 else 2
        return along_t(
            y_send.at[2, place], y_half.at[step // 2], gh_ys.at[slot], gh_yr.at[slot], y_peer(step)
        )

    def finish_resp():
        whole = jnp.where(in_half, fin_own[...], fin_back[...])
        probs = jnp.exp2((resp_scores[...] - whole[0:1]) * factor) * whole[1:2]
        grad_value = dot(probs.astype(BF16), u_rows[...]).astype(BF16)
        resp_score_grads[...] = (probs * (resp_prob_grads[...] - whole[2:3])).astype(BF16)
        grad_key = (dot(resp_score_grads[...], q_rows[...]) * scale).astype(BF16)
        resp_grads[...] = jnp.concatenate([grad_key, grad_value], axis=1)
        for step in (2, 1, 3, 0):
            shard = lax.rem(y + step, 4) * 2 + 1 - core
            sib_send[step] = dot_nt(resp_grads[...], w[shard]).astype(BF16)
            gh_to_sibling(step).start()

    def hidden_terms():
        for step in (2, 1, 3, 0):
            gh_to_sibling(step).wait_recv()
            term = dot_nt(resp_grads[...], w[y_peer(step)]) + sib_recv[step].astype(F32)
            y_send[step] = term.astype(BF16)
            if step == 2:
                gh_half(1).start()
                gh_half(3).start()

    def hidden_onward():
        for step in (1, 3):
            gh_half(step).wait_recv()
            place = pl.ds(0 if step == 1 else half, half)
            both = y_send[step, place].astype(F32) + y_half[step // 2].astype(F32)
            y_send[step, place] = both.astype(BF16)
            gh_to_y(step).start()

    def hidden_sum():
        summed = y_send[0].astype(F32)
        for step in (1, 3):
            gh_from_y(step).wait_recv()
            summed = summed + y_recv[step].astype(F32)
        gh_out[...] = summed.astype(BF16)

    def query_sum(c):
        @pl.when(is_middle)
        def _():
            result_send(c).wait_recv()

        for h in range(c * heads // CHUNKS, (c + 1) * heads // CHUNKS):
            place = pl.ds(h * rows, rows)
            prompt_part = jnp.where(in_half, gq_own[place], gq_back[place]).astype(F32)
            gq = prompt_part + resp_queries[place]
            gq_out[:, pl.ds(h * HD, HD)] = gq.astype(BF16)

    def kept(flag, value):
        return jnp.where(flag, value.astype(F32), 0.0)

    def collect(c):
        @pl.when(is_middle)
        def _():
            pg_far_send(c).wait_recv()
            passed = kept(my_dest == mate, pg_own[c]) + kept(opp_dest == mate, pg_guest[c])
            pg_relay[c] = (passed + kept(far_dest == mate, pg_far[c])).astype(BF16)
            pg_back_send(c).start()

        @pl.when(is_edge)
        def _():
            pg_back_send(c).wait_recv()

        summed = kept(my_dest == r, pg_own[c]) + kept(is_edge, pg_back[c])
        summed = summed + kept(is_middle & (opp_dest == r), pg_guest[c])
        summed = summed + kept(is_middle & (mate_dest == r), pg_edge[c])
        summed = summed + kept(is_middle & (far_dest == r), pg_far[c])
        gp_out[1 - c // CHUNKS, pl.ds((c % CHUNKS) * chunk, chunk)] = summed.astype(BF16)

    @pl.when(is_middle)
    def _():
        stat_send().start()
        pass_on(6, 7)
        for c in range(CHUNKS, total):
            query_send(c).start()
        attend_exponents(scores, local_own)
        for c in range(CHUNKS):
            query_send(c).wait_recv()
        attend_scores(guest_q, guest_part, range(CHUNKS), guest_scores, guest_keys, local_guest)
        pump(4)
        attend_exponents(guest_scores, local_guest)
        attend_values(u_rows, scores, local_own, stat_resp, pg_own, nothing, lambda: pump(5))
        pump(6)
        attend_dot(u_rows, lambda c: middle_part(CHUNKS + c), local_own, fin_own)
        pump(7)
        attend_keys(q_rows, scores, keys, fin_own, pg_own, gq_own, nothing)
        forward(0, 1, 2, 3)
        for c in range(total):
            pass_send(c).wait_send()
            relay_send(c).wait_send()
        stat_send().wait()
        for c in range(CHUNKS, total):
            query_send(c).wait_recv()
        attend_values(guest_u, guest_scores, local_guest, stat_guest, pg_guest, nothing, nothing)
        attend_dot(guest_u, lambda c: guest_part(CHUNKS + c), local_guest, fin_guest)
        fin_send().start()
        attend_keys(
            guest_q, guest_scores, guest_keys, fin_guest, pg_guest, gq_guest,
            lambda c: (forward(CHUNKS + c), collect(c)),
        )
        for c in range(CHUNKS):
            result_send(c).start()
        fin_send().wait()
        finish_resp()
        for c in range(total):
            query_send(c).wait_send()

    @pl.when(is_edge)
    def _():
        attend_scores(q_rows, edge_part, range(CHUNKS), scores, keys, local_own)
        attend_exponents(scores, local_own)
        attend_values(
            u_rows, scores, local_own, stat_resp, pg_own, lambda c: pg_edge_send(c).start(), nothing
        )
        for c in range(total):
            edge_send(c).wait_send()
        attend_dot(u_rows, lambda c: edge_part(CHUNKS + c), local_own, fin_own)
        attend_keys(
            q_rows, scores, keys, fin_own, pg_own, gq_own, lambda c: pg_edge_send(CHUNKS + c).start(),
            finish_resp,
        )

    for step in range(4):
        hid_to_sibling(step).wait_send()
        if step in (1, 3):
            hid_to_y(step).wait_send()
            hid_onward(step).wait_send()

    hidden_terms()

    def resp_query_terms():
        gq_t = dot(resp_kv[:, :HD].T, resp_score_grads[...]) * scale
        for h in range(heads):
            resp_queries[pl.ds(h * rows, rows)] = gq_t[:, h * rows : (h + 1) * rows].T

    @pl.when(is_middle)
    def _():
        collect(4)
        collect(5)
        hidden_onward()
        collect(6)
        resp_query_terms()
        collect(7)
        for c in range(CHUNKS - 1):
            query_sum(c)
        hidden_sum()
        query_sum(CHUNKS - 1)

    @pl.when(is_edge)
    def _():
        resp_query_terms()
        hidden_onward()
        for c in range(CHUNKS):
            query_sum(c)
        for c in range(CHUNKS):
            collect(c)
        hidden_sum()
        for c in range(CHUNKS, total):
            collect(c)

    for step in range(4):
        gh_to_sibling(step).wait_send()
        if step in (1, 3):
            gh_half(step).wait_send()
            gh_to_y(step).wait_send()

    @pl.when(is_edge)
    def _():
        for c in range(total):
            pg_edge_send(c).wait_send()

    @pl.when(is_middle)
    def _():
        for c in range(CHUNKS):
            result_send(c).wait_send()
        for c in range(total):
            pg_far_send(c).wait_send()
            pg_back_send(c).wait_send()


def write_kernel(a_ref, b_ref, c_ref, a_out, b_out, c_out, sems):
    copies = [
        pltpu.make_async_copy(src, dst, sems.at[i])
        for i, (src, dst) in enumerate(((c_ref, c_out), (a_ref, a_out), (b_ref, b_out)))
    ]
    for copy in copies:
        copy.start()
    for copy in copies:
        copy.wait()


def write_out(*arrays):
    anywhere = pl.BlockSpec(memory_space=pl.ANY)
    return pl.pallas_call(
        write_kernel,
        out_shape=tuple(jax.ShapeDtypeStruct(a.shape, a.dtype) for a in arrays),
        in_specs=[anywhere] * 3,
        out_specs=[anywhere] * 3,
        scratch_shapes=[pltpu.SemaphoreType.DMA((3,))],
        compiler_params=pltpu.CompilerParams(vmem_limit_bytes=1024 * 1024),
        name="write_out",
    )(*arrays)


def local(hidden, queries, out_grad, w_key, w_value, prompt_kv, block_dest, resp_len):
    rows, q_cols = queries.shape
    shard_cols = hidden.shape[1]
    shards = w_key.shape[0] // shard_cols
    kv_cols = w_key.shape[1]
    prompt_len = prompt_kv.shape[2]
    chunk = prompt_len // CHUNKS
    total = 2 * CHUNKS
    all_rows = q_cols // HD * rows
    heads = q_cols // HD
    dma = pltpu.SemaphoreType.DMA
    part = pltpu.VMEM((total, chunk, kv_cols), BF16)
    shard = (rows, shard_cols)
    hbm = pl.BlockSpec(memory_space=pltpu.HBM)
    rows_of_heads = pltpu.VMEM((all_rows, HD), BF16)
    stat = pltpu.VMEM((8, all_rows), F32)
    scratch = (
        [part] * 12
        + [rows_of_heads] * 7
        + [
            pltpu.VMEM((prompt_len, HD), BF16),
            pltpu.VMEM((prompt_len, HD), BF16),
            pltpu.VMEM((prompt_len, all_rows), F32),
            pltpu.VMEM((prompt_len, all_rows), F32),
            pltpu.VMEM((prompt_len, all_rows), F32),
            pltpu.VMEM((prompt_len, all_rows), BF16),
            pltpu.VMEM((prompt_len, all_rows), BF16),
            pltpu.VMEM((rows, 2 * HD), BF16),
            pltpu.VMEM((all_rows, HD), F32),
            pltpu.VMEM((rows, all_rows), F32),
            pltpu.VMEM((rows, all_rows), F32),
            pltpu.VMEM((rows, all_rows), BF16),
            pltpu.VMEM((rows, 2 * HD), BF16),
        ]
        + [stat] * 7
        + [
            pltpu.VMEM((shards, shard_cols, 2 * kv_cols), BF16),
            pltpu.VMEM((4, 2) + shard, BF16),
        ]
        + [pltpu.VMEM((4,) + shard, BF16)] * 4
        + [pltpu.VMEM((2, rows // 2, shard_cols), BF16)]
        + [dma((total,))] * 14
        + [dma((CHUNKS,))] * 2
        + [dma((2,))] * 2
        + [dma((4,))] * 8
        + [dma((total,)), dma((2 * heads,)), dma((2,)), dma]
        + [pltpu.SMEM(block_dest.shape, jnp.int32), pltpu.SMEM(resp_len.shape, jnp.int32), dma((2,))]
    )
    grad_query, grad_hidden, grad_prompt = pl.pallas_call(
        kernel,
        out_shape=(
            pltpu.VMEM(queries.shape, BF16),
            pltpu.VMEM(hidden.shape, BF16),
            pltpu.VMEM(prompt_kv.shape[1:], BF16),
        ),
        in_specs=[hbm] * 8,
        out_specs=[pl.BlockSpec(memory_space=pltpu.VMEM)] * 3,
        scratch_shapes=scratch,
        compiler_params=pltpu.CompilerParams(
            collective_id=0, has_side_effects=True, vmem_limit_bytes=60 * 1024 * 1024
        ),
        name="attention_backward",
    )(
        block_dest, resp_len, hidden, queries, out_grad,
        w_key.reshape(shards, shard_cols, kv_cols), w_value.reshape(shards, shard_cols, kv_cols),
        prompt_kv[0],
    )
    return write_out(grad_query, grad_hidden, grad_prompt[None])


def solution(mesh):
    return jax.shard_map(
        local,
        mesh=mesh,
        in_specs=(
            P("dp", "tensor"),
            P("dp", "tensor"),
            P("dp", "tensor"),
            P(None, "tensor"),
            P(None, "tensor"),
            P("dp", None, None, "tensor"),
            P(),
            P(),
        ),
        out_specs=(P("dp", "tensor"), P("dp", "tensor"), P("dp", None, None, "tensor")),
        check_vma=False,
    )
```

```python
import math

import jax
import jax.numpy as jnp
from jax import lax
from jax.experimental import pallas as pl
from jax.experimental.pallas import tpu as pltpu
from jax.sharding import PartitionSpec as P

HD = 128
GROUP = 4
CHUNKS = 4
MESH = pl.DeviceIdType.MESH
BF16 = jnp.bfloat16
F32 = jnp.float32


def dot_nt(a, b):
    return lax.dot_general(a, b, (((1,), (1,)), ((), ())), preferred_element_type=F32)


def dot(a, b):
    return jnp.dot(a, b, preferred_element_type=F32)


def kernel(
    dest_ref, len_ref, hidden_ref, q_ref, u_ref, wk_ref, wv_ref, kv_ref,
    gq_out, gh_out, gp_out,
    own, edge_kv, pass_kv, pass_in, relay_kv, relay_in, pg_own, pg_guest, pg_edge, pg_far, pg_relay, pg_back,
    q_rows, u_rows, guest_q, guest_u, gq_own, gq_guest, gq_back,
    keys, guest_keys, scores, guest_scores, prob_grads, weights, score_grads, resp_kv, resp_queries, resp_scores, resp_prob_grads, resp_score_grads, resp_grads,
    stat_resp, stat_guest, fin_own, fin_guest, fin_back, local_own, local_guest,
    w, hid, sib_send, sib_recv, y_send, y_recv, y_half,
    kv_s, kv_r, q_s, q_r, pass_s, pass_r, relay_s, relay_r, pe_s, pe_r, far_s, far_r, back_s, back_r,
    res_s, res_r, stat_s, stat_r, hid_ys, hid_yr, hid_ss, hid_sr, gh_ss, gh_sr, gh_ys, gh_yr,
    own_sem, qu_sem, w_sem, hid_sem, dests, lengths, small_sem,
):
    rows = q_ref.shape[0]
    heads = q_ref.shape[1] // HD
    all_rows = heads * rows
    prompt_len = kv_ref.shape[1]
    chunk = prompt_len // CHUNKS
    total = 2 * CHUNKS
    scale = 1.0 / math.sqrt(HD)
    factor = scale * math.log2(math.e)
    tile = 64

    me = lax.axis_index("dp")
    r = lax.rem(me, GROUP)
    base = me - r
    mate = r + 1 - 2 * lax.rem(r, 2)
    opp = GROUP - 1 - r
    far = lax.rem(r + 2, GROUP)
    is_edge = (r == 0) | (r == GROUP - 1)
    is_middle = (r == 1) | (r == GROUP - 2)
    tensor = lax.axis_index("tensor")
    core = lax.rem(tensor, 2)
    y = tensor // 2
    sibling = tensor + 1 - 2 * core

    def y_peer(step):
        return lax.rem(y + step, 4) * 2 + core

    def along_z(src, dst, send, recv, place):
        return pltpu.make_async_remote_copy(
            src_ref=src, dst_ref=dst, send_sem=send, recv_sem=recv,
            device_id={"dp": base + place}, device_id_type=MESH,
        )

    def along_t(src, dst, send, recv, place):
        return pltpu.make_async_remote_copy(
            src_ref=src, dst_ref=dst, send_sem=send, recv_sem=recv,
            device_id={"tensor": place}, device_id_type=MESH,
        )

    def kv_part(c):
        return kv_ref.at[c // CHUNKS, pl.ds((c % CHUNKS) * chunk, chunk)]

    def own_copy(c):
        return pltpu.make_async_copy(kv_part(c), own.at[c], own_sem.at[c])

    def q_copy(h):
        span = pl.ds(h * HD, HD)
        return pltpu.make_async_copy(q_ref.at[:, span], q_rows.at[pl.ds(h * rows, rows)], qu_sem.at[h])

    def u_copy(h):
        span = pl.ds(h * HD, HD)
        place = pl.ds(h * rows, rows)
        return pltpu.make_async_copy(u_ref.at[:, span], u_rows.at[place], qu_sem.at[heads + h])

    w_copies = (
        pltpu.make_async_copy(wk_ref, w.at[:, :, pl.ds(0, HD)], w_sem.at[0]),
        pltpu.make_async_copy(wv_ref, w.at[:, :, pl.ds(HD, HD)], w_sem.at[1]),
    )
    hid_copy = pltpu.make_async_copy(hidden_ref, hid.at[0, 0], hid_sem)
    dest_copy = pltpu.make_async_copy(dest_ref, dests, small_sem.at[0])
    len_copy = pltpu.make_async_copy(len_ref, lengths, small_sem.at[1])

    barrier = pltpu.get_barrier_semaphore()
    for step in range(1, GROUP):
        pl.semaphore_signal(
            barrier, inc=1, device_id={"dp": base + lax.rem(r + step, GROUP)}, device_id_type=MESH
        )
        pl.semaphore_signal(
            barrier, inc=1, device_id={"tensor": y_peer(step)}, device_id_type=MESH
        )
    pl.semaphore_signal(barrier, inc=1, device_id={"tensor": sibling}, device_id_type=MESH)

    for h in range(heads):
        q_copy(h).start()
    dest_copy.start()
    len_copy.start()
    for h in range(heads):
        u_copy(h).start()
    hid_copy.start()
    for c in range(total):
        own_copy(c).start()
    for copy in w_copies:
        copy.start()
    for h in range(heads):
        q_copy(h).wait()
    pl.semaphore_wait(barrier, 2 * (GROUP - 1) + 1)

    def edge_send(c):
        return along_z(kv_part(c), edge_kv.at[c], kv_s.at[c], kv_r.at[c], mate)

    def row_part(c):
        return pl.ds(c * (all_rows // CHUNKS), all_rows // CHUNKS)

    def query_send(c):
        src, dst = (q_rows, guest_q) if c < CHUNKS else (u_rows, guest_u)
        place = row_part(c % CHUNKS)
        return along_z(src.at[place], dst.at[place], q_s.at[c], q_r.at[c], opp)

    def pass_send(c):
        return along_z(pass_kv.at[c], pass_in.at[c], pass_s.at[c], pass_r.at[c], opp)

    def relay_send(c):
        return along_z(relay_kv.at[c], relay_in.at[c], relay_s.at[c], relay_r.at[c], mate)

    def stat_send():
        return along_z(stat_resp, stat_guest, stat_s.at[0], stat_r.at[0], opp)

    def fin_send():
        return along_z(fin_guest, fin_back, stat_s.at[1], stat_r.at[1], opp)

    def result_send(c):
        place = row_part(c)
        return along_z(gq_guest.at[place], gq_back.at[place], res_s.at[c], res_r.at[c], opp)

    def pg_edge_send(c):
        return along_z(pg_own.at[c], pg_edge.at[c], pe_s.at[c], pe_r.at[c], mate)

    def pg_far_send(c):
        return along_z(pg_edge.at[c], pg_far.at[c], far_s.at[c], far_r.at[c], opp)

    def pg_back_send(c):
        return along_z(pg_relay.at[c], pg_back.at[c], back_s.at[c], back_r.at[c], mate)

    @pl.when(is_edge)
    def _():
        for c in range(total):
            edge_send(c).start()

    @pl.when(is_middle)
    def _():
        for c in range(2):
            query_send(c).start()

    half = rows // 2

    def hid_to_y(step):
        return along_t(
            hidden_ref, hid.at[4 - step, 0], hid_ys.at[step], hid_yr.at[4 - step], y_peer(step)
        )

    def hid_from_y(step):
        return along_t(hidden_ref, hid.at[step, 0], hid_ys.at[step], hid_yr.at[step], y_peer(step))

    def hid_onward(step):
        place = pl.ds(0 if step == 3 else half, half)
        slot = 0 if step == 3 else 2
        return along_t(
            hid.at[step, 0, place], hid.at[2, 0, place], hid_ys.at[slot], hid_yr.at[slot], y_peer(4 - step)
        )

    def hid_to_sibling(step):
        src = hidden_ref if step == 0 else hid.at[step, 0]
        return along_t(src, hid.at[step, 1], hid_ss.at[step], hid_sr.at[step], sibling)

    for step in (1, 3):
        hid_to_y(step).start()
    hid_to_sibling(0).start()

    dest_copy.wait()
    len_copy.wait()
    my_dest = dests[me] - base
    mate_dest = dests[base + mate] - base
    opp_dest = dests[base + opp] - base
    far_dest = dests[base + far] - base
    length = lengths[me]
    in_half = is_edge | (my_dest == r) | (my_dest == mate)

    for h in range(heads):
        u_copy(h).wait()

    def mask_upstream(h, carry):
        place = pl.ds(h * rows, rows)
        live = lax.broadcasted_iota(jnp.int32, (rows, HD), 0) < length
        u_rows[place] = jnp.where(live, u_rows[place].astype(F32), 0.0).astype(BF16)
        return carry

    lax.fori_loop(0, heads, mask_upstream, 0)
    for c in range(total):
        own_copy(c).wait()

    def attend_scores(q, key_part, chunks, scores, keys, local):
        for c in chunks:
            part = key_part(c)
            span = pl.ds(c * chunk, chunk)
            keys[span] = part
            scores[span] = dot_nt(part, q[...])
            peak = jnp.max(scores[span], axis=0, keepdims=True)
            local[0:1] = peak if c == 0 else jnp.maximum(local[0:1], peak)

    def attend_exponents(scores, local):
        peak = local[0:1]

        def exponents(i, total_sum):
            span = pl.ds(i * tile, tile)
            value = jnp.exp2((scores[span] - peak) * factor)
            scores[span] = value
            return total_sum + jnp.sum(value.reshape(tile // 8, 8, all_rows), axis=0)

        sums = lax.fori_loop(0, prompt_len // tile, exponents, jnp.zeros((8, all_rows), F32))
        local[1:2] = jnp.sum(sums, axis=0, keepdims=True)

    def attend_share(scores, local, stats):
        peak = jnp.maximum(local[0:1], stats[0:1])
        fade = jnp.exp2((local[0:1] - peak) * factor)
        resp_fade = jnp.exp2((stats[0:1] - peak) * factor)
        inverse = 1.0 / (local[1:2] * fade + stats[1:2] * resp_fade)
        share = fade * inverse

        def normalise(i, carry):
            span = pl.ds(i * tile, tile)
            value = scores[span] * share
            scores[span] = value
            weights[span] = value.astype(BF16)
            return carry

        lax.fori_loop(0, prompt_len // tile, normalise, 0)
        local[2:3] = peak
        local[3:4] = inverse
        local[4:5] = stats[2:3] * resp_fade * inverse

    def attend_values(u, pg, after_values):
        for c in range(CHUNKS):
            pg[c] = dot(weights[pl.ds(c * chunk, chunk)], u[...]).astype(BF16)
            after_values(c)

    def attend_dot(u, value_part, local, fin):
        row_dot = local[4:5]
        for c in range(CHUNKS):
            span = pl.ds(c * chunk, chunk)
            grads = dot_nt(value_part(c), u[...])
            prob_grads[span] = grads
            seen = grads * weights[span].astype(F32)
            row_dot = row_dot + jnp.sum(seen, axis=0, keepdims=True)
        fin[0:1] = local[2:3]
        fin[1:2] = local[3:4]
        fin[2:3] = row_dot

    def attend_keys(q, scores, keys, fin, pg, gq, after_keys, before_queries=lambda: None):
        row_dot = fin[2:3]

        def grads_of_scores(i, carry):
            span = pl.ds(i * tile, tile)
            score_grads[span] = (scores[span] * (prob_grads[span] - row_dot)).astype(BF16)
            return carry

        per_chunk = chunk // tile
        for c in range(CHUNKS):
            lax.fori_loop(c * per_chunk, (c + 1) * per_chunk, grads_of_scores, 0)
            part = dot(score_grads[pl.ds(c * chunk, chunk)], q[...]) * scale
            pg[CHUNKS + c] = part.astype(BF16)
            after_keys(c)
        before_queries()
        gq_t = dot(keys[...].T, score_grads[...]) * scale
        for h in range(heads):
            gq[pl.ds(h * rows, rows)] = gq_t[:, h * rows : (h + 1) * rows].T.astype(BF16)

    def nothing(*args):
        pass

    def middle_part(c):
        return jnp.where(my_dest == r, own[c], edge_kv[c])

    def guest_part(c):
        return jnp.where(opp_dest == r, own[c], edge_kv[c])

    def edge_part(c):
        relay_send(c).wait_recv()
        return jnp.where(my_dest == r, own[c], relay_in[c])

    def pass_on(*chunks):
        for c in chunks:
            edge_send(c).wait_recv()
            pass_kv[c] = jnp.where(far_dest == r, own[c], edge_kv[c])
            pass_send(c).start()

    def pump(*chunks):
        for c in chunks:
            pass_send(c).wait_recv()
            relay_kv[c] = jnp.where(mate_dest == r, own[c], pass_in[c])
            relay_send(c).start()

    def forward(*chunks):
        for c in chunks:
            pg_edge_send(c).wait_recv()
            pg_far_send(c).start()

    @pl.when(is_middle)
    def _():
        pass_on(0, 1)
        attend_scores(q_rows, middle_part, (0, 1), scores, keys, local_own)

    hid_copy.wait()
    for copy in w_copies:
        copy.wait()
    for step in (1, 3):
        hid_from_y(step).wait_recv()
        hid_onward(step).start()
        hid_to_sibling(step).start()

    @pl.when(is_middle)
    def _():
        pump(0)
        pass_on(2, 3)
        for c in range(2, CHUNKS):
            query_send(c).start()
        attend_scores(q_rows, middle_part, (2, 3), scores, keys, local_own)
        pump(1)

    resp = dot(hid[0, 0], w[y_peer(0)])
    for step in (1, 3):
        resp = resp + dot(hid[step, 0], w[y_peer(step)])
    for slot in (0, 2):
        place = pl.ds(slot // 2 * half, half)
        along_t(
            hid.at[3 - slot, 0, place], hid.at[2, 0, place], hid_ys.at[slot], hid_yr.at[slot], sibling
        ).wait_recv()
    hid_to_sibling(2).start()

    @pl.when(is_middle)
    def _():
        pump(2)
        pass_on(4, 5)

    resp = resp + dot(hid[2, 0], w[y_peer(2)])
    for step in (0, 1, 3, 2):
        hid_to_sibling(step).wait_recv()
        resp = resp + dot(hid[step, 1], w[lax.rem(y + step, 4) * 2 + 1 - core])
    resp_kv[...] = resp.astype(BF16)

    @pl.when(is_middle)
    def _():
        pump(3)

    key_pos = lax.broadcasted_iota(jnp.int32, (rows, all_rows), 0)
    row_pos = lax.rem(lax.broadcasted_iota(jnp.int32, (rows, all_rows), 1), rows)
    visible = (key_pos <= row_pos) & (key_pos < length)
    resp_scores[...] = jnp.where(visible, dot_nt(resp_kv[:, :HD], q_rows[...]), -1e30)
    resp_prob_grads[...] = dot_nt(resp_kv[:, HD:], u_rows[...])
    resp_peak = jnp.max(resp_scores[...], axis=0, keepdims=True)
    resp_exp = jnp.exp2((resp_scores[...] - resp_peak) * factor)
    stat_resp[0:1] = resp_peak
    stat_resp[1:2] = jnp.sum(resp_exp, axis=0, keepdims=True)
    stat_resp[2:3] = jnp.sum(resp_exp * resp_prob_grads[...], axis=0, keepdims=True)

    def gh_to_sibling(step):
        return along_t(
            sib_send.at[step], sib_recv.at[step], gh_ss.at[step], gh_sr.at[step], sibling
        )

    def gh_to_y(step):
        return along_t(
            y_send.at[step], y_recv.at[4 - step], gh_ys.at[step], gh_yr.at[4 - step], y_peer(step)
        )

    def gh_from_y(step):
        return along_t(
            y_send.at[step], y_recv.at[step], gh_ys.at[step], gh_yr.at[step], y_peer(step)
        )

    def gh_half(step):
        place = pl.ds(0 if step == 1 else half, half)
        slot = 0 if step == 1 else 2
        return along_t(
            y_send.at[2, place], y_half.at[step // 2], gh_ys.at[slot], gh_yr.at[slot], y_peer(step)
        )

    def finish_resp():
        whole = jnp.where(in_half, fin_own[...], fin_back[...])
        probs = jnp.exp2((resp_scores[...] - whole[0:1]) * factor) * whole[1:2]
        grad_value = dot(probs.astype(BF16), u_rows[...]).astype(BF16)
        resp_score_grads[...] = (probs * (resp_prob_grads[...] - whole[2:3])).astype(BF16)
        grad_key = (dot(resp_score_grads[...], q_rows[...]) * scale).astype(BF16)
        resp_grads[...] = jnp.concatenate([grad_key, grad_value], axis=1)
        for step in (2, 1, 3, 0):
            shard = lax.rem(y + step, 4) * 2 + 1 - core
            sib_send[step] = dot_nt(resp_grads[...], w[shard]).astype(BF16)
            gh_to_sibling(step).start()

    def hidden_terms():
        for step in (2, 1, 3, 0):
            gh_to_sibling(step).wait_recv()
            term = dot_nt(resp_grads[...], w[y_peer(step)]) + sib_recv[step].astype(F32)
            y_send[step] = term.astype(BF16)
            if step == 2:
                gh_half(1).start()
                gh_half(3).start()

    def hidden_onward():
        for step in (1, 3):
            gh_half(step).wait_recv()
            place = pl.ds(0 if step == 1 else half, half)
            both = y_send[step, place].astype(F32) + y_half[step // 2].astype(F32)
            y_send[step, place] = both.astype(BF16)
            gh_to_y(step).start()

    def hidden_sum():
        summed = y_send[0].astype(F32)
        for step in (1, 3):
            gh_from_y(step).wait_recv()
            summed = summed + y_recv[step].astype(F32)
        gh_out[...] = summed.astype(BF16)

    def query_sum(c):
        @pl.when(is_middle)
        def _():
            result_send(c).wait_recv()

        for h in range(c * heads // CHUNKS, (c + 1) * heads // CHUNKS):
            place = pl.ds(h * rows, rows)
            prompt_part = jnp.where(in_half, gq_own[place], gq_back[place]).astype(F32)
            gq = prompt_part + resp_queries[place]
            gq_out[:, pl.ds(h * HD, HD)] = gq.astype(BF16)

    def kept(flag, value):
        return jnp.where(flag, value.astype(F32), 0.0)

    def collect(c):
        @pl.when(is_middle)
        def _():
            pg_far_send(c).wait_recv()
            passed = kept(my_dest == mate, pg_own[c]) + kept(opp_dest == mate, pg_guest[c])
            pg_relay[c] = (passed + kept(far_dest == mate, pg_far[c])).astype(BF16)
            pg_back_send(c).start()

        @pl.when(is_edge)
        def _():
            pg_back_send(c).wait_recv()

        summed = kept(my_dest == r, pg_own[c]) + kept(is_edge, pg_back[c])
        summed = summed + kept(is_middle & (opp_dest == r), pg_guest[c])
        summed = summed + kept(is_middle & (mate_dest == r), pg_edge[c])
        summed = summed + kept(is_middle & (far_dest == r), pg_far[c])
        gp_out[1 - c // CHUNKS, pl.ds((c % CHUNKS) * chunk, chunk)] = summed.astype(BF16)

    @pl.when(is_middle)
    def _():
        stat_send().start()
        pass_on(6, 7)
        for c in range(CHUNKS, total):
            query_send(c).start()
        attend_exponents(scores, local_own)
        for c in range(CHUNKS):
            query_send(c).wait_recv()
        attend_scores(guest_q, guest_part, range(CHUNKS), guest_scores, guest_keys, local_guest)
        pump(4)
        attend_exponents(guest_scores, local_guest)
        attend_share(scores, local_own, stat_resp)
        pump(5)
        attend_values(u_rows, pg_own, nothing)
        pump(6)
        attend_dot(u_rows, lambda c: middle_part(CHUNKS + c), local_own, fin_own)
        pump(7)
        attend_keys(q_rows, scores, keys, fin_own, pg_own, gq_own, nothing)
        forward(0, 1)
        stat_send().wait()
        attend_share(guest_scores, local_guest, stat_guest)
        for c in range(total):
            pass_send(c).wait_send()
            relay_send(c).wait_send()
        for c in range(CHUNKS, total):
            query_send(c).wait_recv()
        attend_dot(guest_u, lambda c: guest_part(CHUNKS + c), local_guest, fin_guest)
        fin_send().start()
        forward(2, 3)
        attend_values(guest_u, pg_guest, nothing)
        collect(0)
        collect(1)
        forward(4)
        fin_send().wait()
        forward(5)
        finish_resp()
        forward(6, 7)
        collect(2)
        collect(3)
        hidden_terms()
        attend_keys(
            guest_q, guest_scores, guest_keys, fin_guest, pg_guest, gq_guest,
            lambda c: collect(CHUNKS + c) if c < 2 else None,
        )
        for c in range(CHUNKS):
            result_send(c).start()
        hidden_onward()

    @pl.when(is_edge)
    def _():
        attend_scores(q_rows, edge_part, range(CHUNKS), scores, keys, local_own)
        attend_exponents(scores, local_own)
        attend_share(scores, local_own, stat_resp)
        attend_values(u_rows, pg_own, lambda c: pg_edge_send(c).start())
        for c in range(total):
            edge_send(c).wait_send()
        attend_dot(u_rows, lambda c: edge_part(CHUNKS + c), local_own, fin_own)
        attend_keys(
            q_rows, scores, keys, fin_own, pg_own, gq_own, lambda c: pg_edge_send(CHUNKS + c).start(),
            finish_resp,
        )

    for step in range(4):
        hid_to_sibling(step).wait_send()
        if step in (1, 3):
            hid_to_y(step).wait_send()
            hid_onward(step).wait_send()

    def resp_query_terms():
        gq_t = dot(resp_kv[:, :HD].T, resp_score_grads[...]) * scale
        for h in range(heads):
            resp_queries[pl.ds(h * rows, rows)] = gq_t[:, h * rows : (h + 1) * rows].T

    @pl.when(is_middle)
    def _():
        collect(6)
        collect(7)
        resp_query_terms()
        for c in range(total):
            query_send(c).wait_send()
        for c in range(CHUNKS - 1):
            query_sum(c)
        for c in range(total):
            pg_far_send(c).wait_send()
        hidden_sum()
        for c in range(total - 2):
            pg_back_send(c).wait_send()
        query_sum(CHUNKS - 1)

    @pl.when(is_edge)
    def _():
        hidden_terms()
        resp_query_terms()
        hidden_onward()
        for c in range(CHUNKS):
            query_sum(c)
        for c in range(total):
            pg_edge_send(c).wait_send()
        for c in range(CHUNKS):
            collect(c)
        hidden_sum()
        for c in range(CHUNKS, total):
            collect(c)

    for step in range(4):
        gh_to_sibling(step).wait_send()
        if step in (1, 3):
            gh_half(step).wait_send()
            gh_to_y(step).wait_send()

    @pl.when(is_middle)
    def _():
        for c in range(CHUNKS):
            result_send(c).wait_send()
        for c in range(total - 2, total):
            pg_back_send(c).wait_send()


def write_kernel(a_ref, b_ref, c_ref, a_out, b_out, c_out, sems):
    copies = [
        pltpu.make_async_copy(src, dst, sems.at[i])
        for i, (src, dst) in enumerate(((c_ref, c_out), (a_ref, a_out), (b_ref, b_out)))
    ]
    for copy in copies:
        copy.start()
    for copy in copies:
        copy.wait()


def write_out(*arrays):
    anywhere = pl.BlockSpec(memory_space=pl.ANY)
    return pl.pallas_call(
        write_kernel,
        out_shape=tuple(jax.ShapeDtypeStruct(a.shape, a.dtype) for a in arrays),
        in_specs=[anywhere] * 3,
        out_specs=[anywhere] * 3,
        scratch_shapes=[pltpu.SemaphoreType.DMA((3,))],
        compiler_params=pltpu.CompilerParams(vmem_limit_bytes=1024 * 1024),
        name="write_out",
    )(*arrays)


def local(hidden, queries, out_grad, w_key, w_value, prompt_kv, block_dest, resp_len):
    rows, q_cols = queries.shape
    shard_cols = hidden.shape[1]
    shards = w_key.shape[0] // shard_cols
    kv_cols = w_key.shape[1]
    prompt_len = prompt_kv.shape[2]
    chunk = prompt_len // CHUNKS
    total = 2 * CHUNKS
    all_rows = q_cols // HD * rows
    heads = q_cols // HD
    dma = pltpu.SemaphoreType.DMA
    part = pltpu.VMEM((total, chunk, kv_cols), BF16)
    shard = (rows, shard_cols)
    hbm = pl.BlockSpec(memory_space=pltpu.HBM)
    rows_of_heads = pltpu.VMEM((all_rows, HD), BF16)
    stat = pltpu.VMEM((8, all_rows), F32)
    scratch = (
        [part] * 12
        + [rows_of_heads] * 7
        + [
            pltpu.VMEM((prompt_len, HD), BF16),
            pltpu.VMEM((prompt_len, HD), BF16),
            pltpu.VMEM((prompt_len, all_rows), F32),
            pltpu.VMEM((prompt_len, all_rows), F32),
            pltpu.VMEM((prompt_len, all_rows), F32),
            pltpu.VMEM((prompt_len, all_rows), BF16),
            pltpu.VMEM((prompt_len, all_rows), BF16),
            pltpu.VMEM((rows, 2 * HD), BF16),
            pltpu.VMEM((all_rows, HD), F32),
            pltpu.VMEM((rows, all_rows), F32),
            pltpu.VMEM((rows, all_rows), F32),
            pltpu.VMEM((rows, all_rows), BF16),
            pltpu.VMEM((rows, 2 * HD), BF16),
        ]
        + [stat] * 7
        + [
            pltpu.VMEM((shards, shard_cols, 2 * kv_cols), BF16),
            pltpu.VMEM((4, 2) + shard, BF16),
        ]
        + [pltpu.VMEM((4,) + shard, BF16)] * 4
        + [pltpu.VMEM((2, rows // 2, shard_cols), BF16)]
        + [dma((total,))] * 14
        + [dma((CHUNKS,))] * 2
        + [dma((2,))] * 2
        + [dma((4,))] * 8
        + [dma((total,)), dma((2 * heads,)), dma((2,)), dma]
        + [pltpu.SMEM(block_dest.shape, jnp.int32), pltpu.SMEM(resp_len.shape, jnp.int32), dma((2,))]
    )
    grad_query, grad_hidden, grad_prompt = pl.pallas_call(
        kernel,
        out_shape=(
            pltpu.VMEM(queries.shape, BF16),
            pltpu.VMEM(hidden.shape, BF16),
            pltpu.VMEM(prompt_kv.shape[1:], BF16),
        ),
        in_specs=[hbm] * 8,
        out_specs=[pl.BlockSpec(memory_space=pltpu.VMEM)] * 3,
        scratch_shapes=scratch,
        compiler_params=pltpu.CompilerParams(
            collective_id=0, has_side_effects=True, vmem_limit_bytes=60 * 1024 * 1024
        ),
        name="attention_backward",
    )(
        block_dest, resp_len, hidden, queries, out_grad,
        w_key.reshape(shards, shard_cols, kv_cols), w_value.reshape(shards, shard_cols, kv_cols),
        prompt_kv[0],
    )
    return write_out(grad_query, grad_hidden, grad_prompt[None])


def solution(mesh):
    return jax.shard_map(
        local,
        mesh=mesh,
        in_specs=(
            P("dp", "tensor"),
            P("dp", "tensor"),
            P("dp", "tensor"),
            P(None, "tensor"),
            P(None, "tensor"),
            P("dp", None, None, "tensor"),
            P(),
            P(),
        ),
        out_specs=(P("dp", "tensor"), P("dp", "tensor"), P("dp", None, None, "tensor")),
        check_vma=False,
    )
```

```python
import math

import jax
import jax.numpy as jnp
from jax import lax
from jax.experimental import pallas as pl
from jax.experimental.pallas import tpu as pltpu
from jax.sharding import PartitionSpec as P

HD = 128
GROUP = 4
CHUNKS = 4
MESH = pl.DeviceIdType.MESH
BF16 = jnp.bfloat16
F32 = jnp.float32


def dot_nt(a, b):
    return lax.dot_general(a, b, (((1,), (1,)), ((), ())), preferred_element_type=F32)


def dot(a, b):
    return jnp.dot(a, b, preferred_element_type=F32)


def kernel(
    dest_ref, len_ref, hidden_ref, q_ref, u_ref, wk_ref, wv_ref, kv_ref,
    gq_out, gh_out, gp_out,
    own, edge_kv, pass_kv, pass_in, relay_kv, relay_in, pg_own, pg_guest, pg_edge, pg_far, pg_relay, pg_back,
    q_rows, u_rows, guest_q, guest_u, gq_own, gq_guest, gq_back,
    keys, guest_keys, scores, guest_scores, prob_grads, weights, score_grads, resp_kv, resp_queries, resp_scores, resp_prob_grads, resp_score_grads, resp_grads,
    stat_resp, stat_guest, fin_own, fin_guest, fin_back, local_own, local_guest,
    w, hid, sib_send, sib_recv, y_send, y_recv, y_half,
    kv_s, kv_r, q_s, q_r, pass_s, pass_r, relay_s, relay_r, pe_s, pe_r, far_s, far_r, back_s, back_r,
    res_s, res_r, stat_s, stat_r, hid_ys, hid_yr, hid_ss, hid_sr, gh_ss, gh_sr, gh_ys, gh_yr,
    own_sem, qu_sem, w_sem, hid_sem, dests, lengths, small_sem,
):
    rows = q_ref.shape[0]
    heads = q_ref.shape[1] // HD
    all_rows = heads * rows
    prompt_len = kv_ref.shape[1]
    chunk = prompt_len // CHUNKS
    total = 2 * CHUNKS
    scale = 1.0 / math.sqrt(HD)
    factor = scale * math.log2(math.e)
    tile = 64

    me = lax.axis_index("dp")
    r = lax.rem(me, GROUP)
    base = me - r
    mate = r + 1 - 2 * lax.rem(r, 2)
    opp = GROUP - 1 - r
    far = lax.rem(r + 2, GROUP)
    is_edge = (r == 0) | (r == GROUP - 1)
    is_middle = (r == 1) | (r == GROUP - 2)
    tensor = lax.axis_index("tensor")
    core = lax.rem(tensor, 2)
    y = tensor // 2
    sibling = tensor + 1 - 2 * core

    def y_peer(step):
        return lax.rem(y + step, 4) * 2 + core

    def along_z(src, dst, send, recv, place):
        return pltpu.make_async_remote_copy(
            src_ref=src, dst_ref=dst, send_sem=send, recv_sem=recv,
            device_id={"dp": base + place}, device_id_type=MESH,
        )

    def along_t(src, dst, send, recv, place):
        return pltpu.make_async_remote_copy(
            src_ref=src, dst_ref=dst, send_sem=send, recv_sem=recv,
            device_id={"tensor": place}, device_id_type=MESH,
        )

    def kv_part(c):
        return kv_ref.at[c // CHUNKS, pl.ds((c % CHUNKS) * chunk, chunk)]

    def own_copy(c):
        return pltpu.make_async_copy(kv_part(c), own.at[c], own_sem.at[c])

    def q_copy(h):
        span = pl.ds(h * HD, HD)
        return pltpu.make_async_copy(q_ref.at[:, span], q_rows.at[pl.ds(h * rows, rows)], qu_sem.at[h])

    def u_copy(h):
        span = pl.ds(h * HD, HD)
        place = pl.ds(h * rows, rows)
        return pltpu.make_async_copy(u_ref.at[:, span], u_rows.at[place], qu_sem.at[heads + h])

    w_copies = (
        pltpu.make_async_copy(wk_ref, w.at[:, :, pl.ds(0, HD)], w_sem.at[0]),
        pltpu.make_async_copy(wv_ref, w.at[:, :, pl.ds(HD, HD)], w_sem.at[1]),
    )
    hid_copy = pltpu.make_async_copy(hidden_ref, hid.at[0, 0], hid_sem)
    dest_copy = pltpu.make_async_copy(dest_ref, dests, small_sem.at[0])
    len_copy = pltpu.make_async_copy(len_ref, lengths, small_sem.at[1])

    barrier = pltpu.get_barrier_semaphore()
    for step in range(1, GROUP):
        pl.semaphore_signal(
            barrier, inc=1, device_id={"dp": base + lax.rem(r + step, GROUP)}, device_id_type=MESH
        )
        pl.semaphore_signal(
            barrier, inc=1, device_id={"tensor": y_peer(step)}, device_id_type=MESH
        )
    pl.semaphore_signal(barrier, inc=1, device_id={"tensor": sibling}, device_id_type=MESH)

    for h in range(heads):
        q_copy(h).start()
    dest_copy.start()
    len_copy.start()
    for h in range(heads):
        u_copy(h).start()
    hid_copy.start()
    for c in range(total):
        own_copy(c).start()
    for copy in w_copies:
        copy.start()
    for h in range(heads):
        q_copy(h).wait()
    pl.semaphore_wait(barrier, 2 * (GROUP - 1) + 1)

    def edge_send(c):
        return along_z(kv_part(c), edge_kv.at[c], kv_s.at[c], kv_r.at[c], mate)

    def row_part(c):
        return pl.ds(c * (all_rows // CHUNKS), all_rows // CHUNKS)

    def query_send(c):
        src, dst = (q_rows, guest_q) if c < CHUNKS else (u_rows, guest_u)
        place = row_part(c % CHUNKS)
        return along_z(src.at[place], dst.at[place], q_s.at[c], q_r.at[c], opp)

    def pass_send(c):
        return along_z(pass_kv.at[c], pass_in.at[c], pass_s.at[c], pass_r.at[c], opp)

    def relay_send(c):
        return along_z(relay_kv.at[c], relay_in.at[c], relay_s.at[c], relay_r.at[c], mate)

    def stat_send():
        return along_z(stat_resp, stat_guest, stat_s.at[0], stat_r.at[0], opp)

    def fin_send():
        return along_z(fin_guest, fin_back, stat_s.at[1], stat_r.at[1], opp)

    def result_send(c):
        place = row_part(c)
        return along_z(gq_guest.at[place], gq_back.at[place], res_s.at[c], res_r.at[c], opp)

    def pg_edge_send(c):
        return along_z(pg_own.at[c], pg_edge.at[c], pe_s.at[c], pe_r.at[c], mate)

    def pg_far_send(c):
        return along_z(pg_edge.at[c], pg_far.at[c], far_s.at[c], far_r.at[c], opp)

    def pg_back_send(c):
        return along_z(pg_relay.at[c], pg_back.at[c], back_s.at[c], back_r.at[c], mate)

    @pl.when(is_edge)
    def _():
        for c in range(total):
            edge_send(c).start()

    @pl.when(is_middle)
    def _():
        for c in range(3):
            query_send(c).start()

    half = rows // 2

    def hid_to_y(step):
        return along_t(
            hidden_ref, hid.at[4 - step, 0], hid_ys.at[step], hid_yr.at[4 - step], y_peer(step)
        )

    def hid_from_y(step):
        return along_t(hidden_ref, hid.at[step, 0], hid_ys.at[step], hid_yr.at[step], y_peer(step))

    def hid_onward(step):
        place = pl.ds(0 if step == 3 else half, half)
        slot = 0 if step == 3 else 2
        return along_t(
            hid.at[step, 0, place], hid.at[2, 0, place], hid_ys.at[slot], hid_yr.at[slot], y_peer(4 - step)
        )

    def hid_to_sibling(step):
        src = hidden_ref if step == 0 else hid.at[step, 0]
        return along_t(src, hid.at[step, 1], hid_ss.at[step], hid_sr.at[step], sibling)

    for step in (1, 3):
        hid_to_y(step).start()
    hid_to_sibling(0).start()

    dest_copy.wait()
    len_copy.wait()
    my_dest = dests[me] - base
    mate_dest = dests[base + mate] - base
    opp_dest = dests[base + opp] - base
    far_dest = dests[base + far] - base
    length = lengths[me]
    in_half = is_edge | (my_dest == r) | (my_dest == mate)

    for h in range(heads):
        u_copy(h).wait()

    def mask_upstream(h, carry):
        place = pl.ds(h * rows, rows)
        live = lax.broadcasted_iota(jnp.int32, (rows, HD), 0) < length
        u_rows[place] = jnp.where(live, u_rows[place].astype(F32), 0.0).astype(BF16)
        return carry

    lax.fori_loop(0, heads, mask_upstream, 0)
    for c in range(total):
        own_copy(c).wait()

    def attend_scores(q, key_part, chunks, scores, keys, local):
        for c in chunks:
            part = key_part(c)
            span = pl.ds(c * chunk, chunk)
            keys[span] = part
            scores[span] = dot_nt(part, q[...])
            peak = jnp.max(scores[span], axis=0, keepdims=True)
            local[0:1] = peak if c == 0 else jnp.maximum(local[0:1], peak)

    def attend_exponents(scores, local):
        peak = local[0:1]

        def exponents(i, total_sum):
            span = pl.ds(i * tile, tile)
            value = jnp.exp2((scores[span] - peak) * factor)
            scores[span] = value
            return total_sum + jnp.sum(value.reshape(tile // 8, 8, all_rows), axis=0)

        sums = lax.fori_loop(0, prompt_len // tile, exponents, jnp.zeros((8, all_rows), F32))
        local[1:2] = jnp.sum(sums, axis=0, keepdims=True)

    def attend_share(scores, local, stats):
        peak = jnp.maximum(local[0:1], stats[0:1])
        fade = jnp.exp2((local[0:1] - peak) * factor)
        resp_fade = jnp.exp2((stats[0:1] - peak) * factor)
        inverse = 1.0 / (local[1:2] * fade + stats[1:2] * resp_fade)
        share = fade * inverse

        def normalise(i, carry):
            span = pl.ds(i * tile, tile)
            value = scores[span] * share
            scores[span] = value
            weights[span] = value.astype(BF16)
            return carry

        lax.fori_loop(0, prompt_len // tile, normalise, 0)
        local[2:3] = peak
        local[3:4] = inverse
        local[4:5] = stats[2:3] * resp_fade * inverse

    def attend_values(u, pg, after_values):
        for c in range(CHUNKS):
            pg[c] = dot(weights[pl.ds(c * chunk, chunk)], u[...]).astype(BF16)
            after_values(c)

    def attend_dot(u, value_part, local, fin, parts=1, before=lambda part: None):
        for part in range(parts):
            before(part)
            place = pl.ds(part * (all_rows // parts), all_rows // parts)
            row_dot = local[4:5, place]
            for c in range(CHUNKS):
                span = pl.ds(c * chunk, chunk)
                grads = dot_nt(value_part(c), u[place])
                prob_grads[span, place] = grads
                seen = grads * weights[span, place].astype(F32)
                row_dot = row_dot + jnp.sum(seen, axis=0, keepdims=True)
            fin[2:3, place] = row_dot
        fin[0:1] = local[2:3]
        fin[1:2] = local[3:4]

    def attend_keys(q, scores, keys, fin, pg, gq, after_keys, before_queries=lambda: None):
        row_dot = fin[2:3]

        def grads_of_scores(i, carry):
            span = pl.ds(i * tile, tile)
            score_grads[span] = (scores[span] * (prob_grads[span] - row_dot)).astype(BF16)
            return carry

        per_chunk = chunk // tile
        for c in range(CHUNKS):
            lax.fori_loop(c * per_chunk, (c + 1) * per_chunk, grads_of_scores, 0)
            part = dot(score_grads[pl.ds(c * chunk, chunk)], q[...]) * scale
            pg[CHUNKS + c] = part.astype(BF16)
            after_keys(c)
        before_queries()
        gq_t = dot(keys[...].T, score_grads[...]) * scale
        for h in range(heads):
            gq[pl.ds(h * rows, rows)] = gq_t[:, h * rows : (h + 1) * rows].T.astype(BF16)

    def nothing(*args):
        pass

    def middle_part(c):
        return jnp.where(my_dest == r, own[c], edge_kv[c])

    def guest_part(c):
        return jnp.where(opp_dest == r, own[c], edge_kv[c])

    def edge_part(c):
        relay_send(c).wait_recv()
        return jnp.where(my_dest == r, own[c], relay_in[c])

    def pass_on(*chunks):
        for c in chunks:
            edge_send(c).wait_recv()
            pass_kv[c] = jnp.where(far_dest == r, own[c], edge_kv[c])
            pass_send(c).start()

    def pump(*chunks):
        for c in chunks:
            pass_send(c).wait_recv()
            relay_kv[c] = jnp.where(mate_dest == r, own[c], pass_in[c])
            relay_send(c).start()

    def forward(*chunks):
        for c in chunks:
            pg_edge_send(c).wait_recv()
            pg_far_send(c).start()

    @pl.when(is_middle)
    def _():
        pass_on(0, 1)
        attend_scores(q_rows, middle_part, (0, 1), scores, keys, local_own)

    hid_copy.wait()
    for copy in w_copies:
        copy.wait()
    for step in (1, 3):
        hid_from_y(step).wait_recv()
        hid_onward(step).start()
        hid_to_sibling(step).start()

    @pl.when(is_middle)
    def _():
        pump(0)
        pass_on(2, 3)
        query_send(3).start()
        attend_scores(q_rows, middle_part, (2, 3), scores, keys, local_own)
        pump(1)

    resp = dot(hid[0, 0], w[y_peer(0)])
    for step in (1, 3):
        resp = resp + dot(hid[step, 0], w[y_peer(step)])
    for slot in (0, 2):
        place = pl.ds(slot // 2 * half, half)
        along_t(
            hid.at[3 - slot, 0, place], hid.at[2, 0, place], hid_ys.at[slot], hid_yr.at[slot], sibling
        ).wait_recv()
    hid_to_sibling(2).start()

    @pl.when(is_middle)
    def _():
        pump(2)
        pass_on(4, 5)

    resp = resp + dot(hid[2, 0], w[y_peer(2)])
    for step in (0, 1, 3, 2):
        hid_to_sibling(step).wait_recv()
        resp = resp + dot(hid[step, 1], w[lax.rem(y + step, 4) * 2 + 1 - core])
    resp_kv[...] = resp.astype(BF16)

    @pl.when(is_middle)
    def _():
        pump(3)

    key_pos = lax.broadcasted_iota(jnp.int32, (rows, all_rows), 0)
    row_pos = lax.rem(lax.broadcasted_iota(jnp.int32, (rows, all_rows), 1), rows)
    visible = (key_pos <= row_pos) & (key_pos < length)
    resp_scores[...] = jnp.where(visible, dot_nt(resp_kv[:, :HD], q_rows[...]), -1e30)
    resp_prob_grads[...] = dot_nt(resp_kv[:, HD:], u_rows[...])
    resp_peak = jnp.max(resp_scores[...], axis=0, keepdims=True)
    resp_exp = jnp.exp2((resp_scores[...] - resp_peak) * factor)
    stat_resp[0:1] = resp_peak
    stat_resp[1:2] = jnp.sum(resp_exp, axis=0, keepdims=True)
    stat_resp[2:3] = jnp.sum(resp_exp * resp_prob_grads[...], axis=0, keepdims=True)

    def gh_to_sibling(step):
        return along_t(
            sib_send.at[step], sib_recv.at[step], gh_ss.at[step], gh_sr.at[step], sibling
        )

    def gh_to_y(step):
        return along_t(
            y_send.at[step], y_recv.at[4 - step], gh_ys.at[step], gh_yr.at[4 - step], y_peer(step)
        )

    def gh_from_y(step):
        return along_t(
            y_send.at[step], y_recv.at[step], gh_ys.at[step], gh_yr.at[step], y_peer(step)
        )

    def gh_half(step):
        place = pl.ds(0 if step == 1 else half, half)
        slot = 0 if step == 1 else 2
        return along_t(
            y_send.at[2, place], y_half.at[step // 2], gh_ys.at[slot], gh_yr.at[slot], y_peer(step)
        )

    def finish_resp():
        whole = jnp.where(in_half, fin_own[...], fin_back[...])
        probs = jnp.exp2((resp_scores[...] - whole[0:1]) * factor) * whole[1:2]
        grad_value = dot(probs.astype(BF16), u_rows[...]).astype(BF16)
        resp_score_grads[...] = (probs * (resp_prob_grads[...] - whole[2:3])).astype(BF16)
        grad_key = (dot(resp_score_grads[...], q_rows[...]) * scale).astype(BF16)
        resp_grads[...] = jnp.concatenate([grad_key, grad_value], axis=1)
        for step in (2, 1, 3, 0):
            shard = lax.rem(y + step, 4) * 2 + 1 - core
            sib_send[step] = dot_nt(resp_grads[...], w[shard]).astype(BF16)
            gh_to_sibling(step).start()

    def hidden_terms():
        for step in (2, 1, 3, 0):
            gh_to_sibling(step).wait_recv()
            term = dot_nt(resp_grads[...], w[y_peer(step)]) + sib_recv[step].astype(F32)
            y_send[step] = term.astype(BF16)
            if step == 2:
                gh_half(1).start()
                gh_half(3).start()

    def hidden_onward():
        for step in (1, 3):
            gh_half(step).wait_recv()
            place = pl.ds(0 if step == 1 else half, half)
            both = y_send[step, place].astype(F32) + y_half[step // 2].astype(F32)
            y_send[step, place] = both.astype(BF16)
            gh_to_y(step).start()

    def hidden_sum():
        summed = y_send[0].astype(F32)
        for step in (1, 3):
            gh_from_y(step).wait_recv()
            summed = summed + y_recv[step].astype(F32)
        gh_out[...] = summed.astype(BF16)

    def query_sum(c):
        @pl.when(is_middle)
        def _():
            result_send(c).wait_recv()

        for h in range(c * heads // CHUNKS, (c + 1) * heads // CHUNKS):
            place = pl.ds(h * rows, rows)
            prompt_part = jnp.where(in_half, gq_own[place], gq_back[place]).astype(F32)
            gq = prompt_part + resp_queries[place]
            gq_out[:, pl.ds(h * HD, HD)] = gq.astype(BF16)

    def kept(flag, value):
        return jnp.where(flag, value.astype(F32), 0.0)

    def collect(c):
        @pl.when(is_middle)
        def _():
            pg_far_send(c).wait_recv()
            passed = kept(my_dest == mate, pg_own[c]) + kept(opp_dest == mate, pg_guest[c])
            pg_relay[c] = (passed + kept(far_dest == mate, pg_far[c])).astype(BF16)
            pg_back_send(c).start()

        @pl.when(is_edge)
        def _():
            pg_back_send(c).wait_recv()

        summed = kept(my_dest == r, pg_own[c]) + kept(is_edge, pg_back[c])
        summed = summed + kept(is_middle & (opp_dest == r), pg_guest[c])
        summed = summed + kept(is_middle & (mate_dest == r), pg_edge[c])
        summed = summed + kept(is_middle & (far_dest == r), pg_far[c])
        gp_out[1 - c // CHUNKS, pl.ds((c % CHUNKS) * chunk, chunk)] = summed.astype(BF16)

    @pl.when(is_middle)
    def _():
        stat_send().start()
        pass_on(6, 7)
        for c in range(CHUNKS, total):
            query_send(c).start()
        attend_exponents(scores, local_own)
        for c in range(CHUNKS):
            query_send(c).wait_recv()
        attend_scores(guest_q, guest_part, range(CHUNKS), guest_scores, guest_keys, local_guest)
        pump(4)
        attend_exponents(guest_scores, local_guest)
        attend_share(scores, local_own, stat_resp)
        pump(5)
        attend_values(u_rows, pg_own, nothing)
        pump(6)
        attend_dot(u_rows, lambda c: middle_part(CHUNKS + c), local_own, fin_own)
        pump(7)
        attend_keys(q_rows, scores, keys, fin_own, pg_own, gq_own, nothing)
        forward(0, 1)
        stat_send().wait()
        attend_share(guest_scores, local_guest, stat_guest)
        for c in range(total):
            pass_send(c).wait_send()
            relay_send(c).wait_send()
        attend_dot(
            guest_u, lambda c: guest_part(CHUNKS + c), local_guest, fin_guest,
            CHUNKS, lambda part: query_send(CHUNKS + part).wait_recv(),
        )
        fin_send().start()
        forward(2, 3)
        attend_values(guest_u, pg_guest, nothing)
        collect(0)
        collect(1)
        forward(4)
        fin_send().wait()
        forward(5)
        finish_resp()
        forward(6, 7)
        collect(2)
        collect(3)
        hidden_terms()
        attend_keys(
            guest_q, guest_scores, guest_keys, fin_guest, pg_guest, gq_guest,
            lambda c: collect(CHUNKS + c) if c < 2 else None,
        )
        for c in range(CHUNKS):
            result_send(c).start()
        hidden_onward()

    @pl.when(is_edge)
    def _():
        attend_scores(q_rows, edge_part, range(CHUNKS), scores, keys, local_own)
        attend_exponents(scores, local_own)
        attend_share(scores, local_own, stat_resp)
        attend_values(u_rows, pg_own, lambda c: pg_edge_send(c).start())
        for c in range(total):
            edge_send(c).wait_send()
        attend_dot(u_rows, lambda c: edge_part(CHUNKS + c), local_own, fin_own)
        attend_keys(
            q_rows, scores, keys, fin_own, pg_own, gq_own, lambda c: pg_edge_send(CHUNKS + c).start(),
            finish_resp,
        )

    for step in range(4):
        hid_to_sibling(step).wait_send()
        if step in (1, 3):
            hid_to_y(step).wait_send()
            hid_onward(step).wait_send()

    def resp_query_terms():
        gq_t = dot(resp_kv[:, :HD].T, resp_score_grads[...]) * scale
        for h in range(heads):
            resp_queries[pl.ds(h * rows, rows)] = gq_t[:, h * rows : (h + 1) * rows].T

    @pl.when(is_middle)
    def _():
        collect(6)
        collect(7)
        resp_query_terms()
        for c in range(total):
            query_send(c).wait_send()
        for c in range(CHUNKS - 1):
            query_sum(c)
        for c in range(total):
            pg_far_send(c).wait_send()
        hidden_sum()
        for c in range(total - 2):
            pg_back_send(c).wait_send()
        query_sum(CHUNKS - 1)

    @pl.when(is_edge)
    def _():
        hidden_terms()
        resp_query_terms()
        hidden_onward()
        for c in range(CHUNKS):
            query_sum(c)
        for c in range(total):
            pg_edge_send(c).wait_send()
        for c in range(CHUNKS):
            collect(c)
        hidden_sum()
        for c in range(CHUNKS, total):
            collect(c)

    for step in range(4):
        gh_to_sibling(step).wait_send()
        if step in (1, 3):
            gh_half(step).wait_send()
            gh_to_y(step).wait_send()

    @pl.when(is_middle)
    def _():
        for c in range(CHUNKS):
            result_send(c).wait_send()
        for c in range(total - 2, total):
            pg_back_send(c).wait_send()


def write_kernel(a_ref, b_ref, c_ref, a_out, b_out, c_out, sems):
    copies = [
        pltpu.make_async_copy(src, dst, sems.at[i])
        for i, (src, dst) in enumerate(((c_ref, c_out), (a_ref, a_out), (b_ref, b_out)))
    ]
    for copy in copies:
        copy.start()
    for copy in copies:
        copy.wait()


def write_out(*arrays):
    anywhere = pl.BlockSpec(memory_space=pl.ANY)
    return pl.pallas_call(
        write_kernel,
        out_shape=tuple(jax.ShapeDtypeStruct(a.shape, a.dtype) for a in arrays),
        in_specs=[anywhere] * 3,
        out_specs=[anywhere] * 3,
        scratch_shapes=[pltpu.SemaphoreType.DMA((3,))],
        compiler_params=pltpu.CompilerParams(vmem_limit_bytes=1024 * 1024),
        name="write_out",
    )(*arrays)


def local(hidden, queries, out_grad, w_key, w_value, prompt_kv, block_dest, resp_len):
    rows, q_cols = queries.shape
    shard_cols = hidden.shape[1]
    shards = w_key.shape[0] // shard_cols
    kv_cols = w_key.shape[1]
    prompt_len = prompt_kv.shape[2]
    chunk = prompt_len // CHUNKS
    total = 2 * CHUNKS
    all_rows = q_cols // HD * rows
    heads = q_cols // HD
    dma = pltpu.SemaphoreType.DMA
    part = pltpu.VMEM((total, chunk, kv_cols), BF16)
    shard = (rows, shard_cols)
    hbm = pl.BlockSpec(memory_space=pltpu.HBM)
    rows_of_heads = pltpu.VMEM((all_rows, HD), BF16)
    stat = pltpu.VMEM((8, all_rows), F32)
    scratch = (
        [part] * 12
        + [rows_of_heads] * 7
        + [
            pltpu.VMEM((prompt_len, HD), BF16),
            pltpu.VMEM((prompt_len, HD), BF16),
            pltpu.VMEM((prompt_len, all_rows), F32),
            pltpu.VMEM((prompt_len, all_rows), F32),
            pltpu.VMEM((prompt_len, all_rows), F32),
            pltpu.VMEM((prompt_len, all_rows), BF16),
            pltpu.VMEM((prompt_len, all_rows), BF16),
            pltpu.VMEM((rows, 2 * HD), BF16),
            pltpu.VMEM((all_rows, HD), F32),
            pltpu.VMEM((rows, all_rows), F32),
            pltpu.VMEM((rows, all_rows), F32),
            pltpu.VMEM((rows, all_rows), BF16),
            pltpu.VMEM((rows, 2 * HD), BF16),
        ]
        + [stat] * 7
        + [
            pltpu.VMEM((shards, shard_cols, 2 * kv_cols), BF16),
            pltpu.VMEM((4, 2) + shard, BF16),
        ]
        + [pltpu.VMEM((4,) + shard, BF16)] * 4
        + [pltpu.VMEM((2, rows // 2, shard_cols), BF16)]
        + [dma((total,))] * 14
        + [dma((CHUNKS,))] * 2
        + [dma((2,))] * 2
        + [dma((4,))] * 8
        + [dma((total,)), dma((2 * heads,)), dma((2,)), dma]
        + [pltpu.SMEM(block_dest.shape, jnp.int32), pltpu.SMEM(resp_len.shape, jnp.int32), dma((2,))]
    )
    grad_query, grad_hidden, grad_prompt = pl.pallas_call(
        kernel,
        out_shape=(
            pltpu.VMEM(queries.shape, BF16),
            pltpu.VMEM(hidden.shape, BF16),
            pltpu.VMEM(prompt_kv.shape[1:], BF16),
        ),
        in_specs=[hbm] * 8,
        out_specs=[pl.BlockSpec(memory_space=pltpu.VMEM)] * 3,
        scratch_shapes=scratch,
        compiler_params=pltpu.CompilerParams(
            collective_id=0, has_side_effects=True, vmem_limit_bytes=60 * 1024 * 1024
        ),
        name="attention_backward",
    )(
        block_dest, resp_len, hidden, queries, out_grad,
        w_key.reshape(shards, shard_cols, kv_cols), w_value.reshape(shards, shard_cols, kv_cols),
        prompt_kv[0],
    )
    return write_out(grad_query, grad_hidden, grad_prompt[None])


def solution(mesh):
    return jax.shard_map(
        local,
        mesh=mesh,
        in_specs=(
            P("dp", "tensor"),
            P("dp", "tensor"),
            P("dp", "tensor"),
            P(None, "tensor"),
            P(None, "tensor"),
            P("dp", None, None, "tensor"),
            P(),
            P(),
        ),
        out_specs=(P("dp", "tensor"), P("dp", "tensor"), P("dp", None, None, "tensor")),
        check_vma=False,
    )
```
